32 devices in a mesh: leaf: 8 (over z, x), rhs: 4 (over y, core).
Axes of the slice: x: 2, y: 2, z: 4, core: 2. Of those that a mesh axis runs over, the one named last changes fastest.
Arguments:
- fields: bfloat16 [16384, 1024], P('leaf', 'rhs'), may hold values from -6 to 6
- owner: int32 [16384, 1], P('leaf'), may hold values from 0 to 7; in each aligned block of 2048 rows (0 to 2047, 2048 to 4095, ...) at most 512 rows name the same one
- source_basis: bfloat16 [16384, 256], P('leaf'), may hold values from -0.125 to 0.125
- field_basis: bfloat16 [16384, 256], P('leaf'), may hold values from -0.375 to 0.375
- transfer: bfloat16 [8, 3, 256, 512], P('leaf', None, 'rhs'), may hold values from -0.25 to 0.25
- near_blocks: bfloat16 [64, 7, 256, 256], P('leaf'), may hold values from -0.25 to 0.25
- near_index: int32 [64, 7], P('leaf'), may hold values from 0 to 7
- near_count: int32 [64], P('leaf'), may hold values from 1 to 7
Outputs:
- scattered: bfloat16 [16384, 1024], P('leaf', 'rhs')
The draws below stay inside these ranges and needn't reach their ends.
Inputs may be any that keep to these rules, and one draw needn't show every extreme that they name: In the rows of one group of 2048 rows at most 512 name one owner; in some group one owner is named by exactly 512. `near_index`: Row-block numbers counted within the same group of 8 row blocks.
All inputs are finite; a program needn't handle non-finite values.
Results may differ from the reference program's by a relative error of at most 0.006.
Values may be sent and summed in bfloat16 or wider, within the bound.
No kernel may reach another device: no remote copies, remote signals or barrier semaphores. Data moves between devices by JAX's collectives and lax.ppermute only.
A program may use at most 128 MiB of HBM per device.

```python
import math
import jax
import jax.numpy as jnp
import numpy as np
from jax import lax

K = 256
LEVELS = 3
BLK = 256
NEAR = 7
ROWS_DEV = 2048
COLS = 1024
ROWS = 16384
CAP = 512
BPD = 8
BLOCKS = 64
N_LEAF = 8


def draw_near_count(key, part):
    counts = jax.random.randint(key, (BLOCKS,), 1, NEAR + 1, dtype=jnp.int32)
    chosen_spots = jax.random.randint(jax.random.fold_in(key, 11), (2,), 0, BLOCKS, dtype=jnp.int32)
    second_spot = (chosen_spots[0] + 1 + chosen_spots[1] % (BLOCKS - 1)) % BLOCKS
    places = jnp.arange(BLOCKS, dtype=jnp.int32)
    counts = jnp.where(places == chosen_spots[0], NEAR, counts)
    counts = jnp.where(places == second_spot, 1, counts)
    return counts.astype(jnp.int32)


def touch_ends(array, rng, least, largest):
    spot = [jax.random.randint(jax.random.fold_in(rng, axis), (), 0, length) for axis, length in enumerate(array.shape)]
    widest = array.shape.index(max(array.shape))
    neighbour = spot[:widest] + [(spot[widest] + 1) % array.shape[widest]] + spot[widest + 1:]
    return array.at[tuple(spot)].set(least).at[tuple(neighbour)].set(largest)


def levels(own_key, dims, split, smallest, largest):
    def one(dim, parts):
        steps = jax.random.uniform(jax.random.fold_in(jax.random.fold_in(own_key, 6), dim), (parts,), jnp.float32, smallest / len(split), largest / len(split))
        return jnp.repeat(jnp.exp(steps), dims[dim] // parts).reshape((-1,) + (1,) * (len(dims) - dim - 1))

    level = one(*split[0])
    for cut in split[1:]:
        level = level * one(*cut)
    return level


def shared_out(own_key, own, number, rows, number_of, top, reach, skew):
    order = jax.random.permutation(own_key, number_of)
    crowded, ordinary = shares(number_of, rows * top, reach, skew, True), shares(number_of, rows * top, reach, skew, False)
    places = jnp.arange(number_of)

    def named(sizes, offset_by):
        used = int((sizes > 0).sum())
        fixed = max(1, used // 4)
        shifted = fixed + (places - fixed + offset_by * (used - fixed)) % max(1, number_of - fixed)
        return jnp.zeros((number_of,), jnp.int32).at[order[jnp.where(places < fixed, places, shifted)]].set(jnp.asarray(sizes, jnp.int32))

    sizes = jnp.where(number % 4 == 0, named(crowded, number // 4), named(ordinary, number - number // 4 - 1))
    mixed = jax.random.permutation(jax.random.fold_in(own, 3), number_of)
    donor, receiver = mixed[0:number_of // 2 * 2:2], mixed[1:number_of // 2 * 2:2]
    room = jnp.minimum(sizes[donor] - 1, reach - sizes[receiver]) // 2
    room = jnp.where((donor == order[0]) | (receiver == order[0]) | (sizes[receiver] == 0), 0, jnp.maximum(room, 0))
    shifted = jax.random.randint(jax.random.fold_in(own, 4), (number_of // 2,), 0, 1 << 20) % (room + 1)
    sizes = sizes.at[donor].add(-shifted).at[receiver].add(shifted)
    labels = jnp.searchsorted(jnp.cumsum(sizes), jnp.arange(rows * top), side="right").astype(jnp.int32)
    table = labels.reshape(top, rows).T
    table = table[jax.random.permutation(jax.random.fold_in(own, 1), rows)]
    offset_by = jax.random.randint(jax.random.fold_in(own, 2), (rows, 1), 0, top)
    return jnp.take_along_axis(table, (jnp.arange(top)[None, :] + offset_by) % top, axis=1)


def shares(count, total, bound, lean, full):
    loads = [(1 << 20) // math.isqrt(standing ** lean) + 1 for standing in range(1, count + 1)]
    largest = bound if full else min(bound, max(-(-total // count), total * loads[0] // sum(loads)))
    least = 1 if total - largest >= count - 1 else 0
    given, surplus = [largest] + [least] * (count - 1), total - largest - least * (count - 1)
    while surplus > 0:
        movable = [i for i in range(1, count) if given[i] < largest] or [i for i in range(1, count) if given[i] < bound]
        pool, remaining = sum([loads[i] for i in movable]), surplus
        for i in movable:
            extra = min(bound - given[i], max(1, remaining * loads[i] // pool), surplus)
            given[i] = given[i] + extra
            surplus = surplus - extra
    return np.array(given)


def scatter_about(rng, extent, width, bound, pieces=(), kind=jnp.bfloat16):
    values = jax.random.normal(rng, extent, jnp.float32) * width
    if len(pieces) > 0:
        values = levels(rng, extent, pieces, -0.22, 0.18) * values
    return jnp.clip(values, min=-bound, max=bound).astype(kind)


def setup_inputs(seed: int = 0) -> dict:
    keys = jax.random.split(jax.random.key(seed), 9)
    fields = scatter_about(keys[0], (ROWS, COLS), 1.0, 6.0, ((0, 8), (1, 4)))
    owner_keys = jax.random.split(jax.random.fold_in(keys[1], 1), ROWS // ROWS_DEV)
    owner_turns = jax.random.permutation(jax.random.fold_in(keys[1], 3), ROWS // ROWS_DEV)
    owner = jax.vmap(lambda own, number: shared_out(jax.random.fold_in(keys[1], 2), own, number, ROWS_DEV, N_LEAF, 1, CAP, 2))(owner_keys, owner_turns).reshape((ROWS, 1))
    source_basis = scatter_about(keys[2], (ROWS, K), ROWS_DEV ** -0.5, 0.125, ((0, 8),))
    field_basis = scatter_about(keys[3], (ROWS, K), K ** -0.5, 0.375, ((0, 8),))
    transfer = scatter_about(keys[4], (N_LEAF, LEVELS, K, 2 * K), (2 * K) ** -0.5, 0.25, ((0, 8), (2, 4)))
    near_blocks = scatter_about(keys[5], (BLOCKS, NEAR, BLK, BLK), (2 * BLK) ** -0.5, 0.25, ((0, 8),))
    near_index = touch_ends(jax.random.randint(keys[6], (BLOCKS, NEAR), 0, BPD), jax.random.fold_in(keys[6], 1), 0, BPD - 1).astype(jnp.int32)
    near_count = draw_near_count(jax.random.fold_in(keys[8], 71), 0)
    return dict(fields=fields, owner=owner, source_basis=source_basis, field_basis=field_basis, transfer=transfer, near_blocks=near_blocks, near_index=near_index, near_count=near_count)


def slot_numbers(owners_of):
    onehot = (owners_of[:, None] == jnp.arange(N_LEAF, dtype=jnp.int32)[None, :]).astype(jnp.int32)
    before = jnp.cumsum(onehot, axis=0) - onehot
    rank_in = jnp.sum(before * onehot, axis=1)
    return (owners_of * CAP + rank_in).astype(jnp.int32)


def reference(fields, owner, source_basis, field_basis, transfer, near_blocks, near_index, near_count):
    col_count = fields.shape[1]
    x_groups = fields.reshape(N_LEAF, ROWS_DEV, col_count)
    owner_groups = owner[:, 0].reshape(N_LEAF, ROWS_DEV)
    source_groups = source_basis.reshape(N_LEAF, ROWS_DEV, K)
    field_groups = field_basis.reshape(N_LEAF, ROWS_DEV, K)

    def add_source(totals, inputs):
        x_one, owner_one, source_one = inputs
        slot_index = slot_numbers(owner_one)
        x_slots = jnp.zeros((N_LEAF * CAP, col_count), jnp.float32).at[slot_index].set(x_one.astype(jnp.float32))
        v_slots = jnp.zeros((N_LEAF * CAP, K), jnp.float32).at[slot_index].set(source_one.astype(jnp.float32))
        terms = jnp.einsum('bck,bcn->bkn', v_slots.reshape(N_LEAF, CAP, K), x_slots.reshape(N_LEAF, CAP, col_count))
        return totals + terms, None

    totals, _ = lax.scan(add_source, jnp.zeros((N_LEAF, K, col_count), jnp.float32), (x_groups, owner_groups, source_groups))
    coefficients = totals.astype(jnp.bfloat16)
    for level_num in range(LEVELS):
        stride = 2 ** level_num
        paired = coefficients.reshape(N_LEAF // (2 * stride), 2, stride, K, col_count)[:, ::-1].reshape(N_LEAF, K, col_count)
        stacked = jnp.concatenate([coefficients, paired], axis=1).astype(jnp.float32)
        coefficients = jnp.einsum('bij,bjn->bin', transfer[:, level_num].astype(jnp.float32), stacked).astype(jnp.bfloat16)
    final_coeffs = coefficients.astype(jnp.float32)

    index_groups = near_index.reshape(N_LEAF, BPD, NEAR)
    count_groups = near_count.reshape(N_LEAF, BPD)
    block_groups = near_blocks.reshape(N_LEAF, BPD, NEAR, BLK, BLK)

    def one_device(inputs):
        x_one, owner_one, field_one, block_weights, index_one, count_one = inputs
        slot_index = slot_numbers(owner_one)
        u_slots = jnp.zeros((N_LEAF * CAP, K), jnp.float32).at[slot_index].set(field_one.astype(jnp.float32))
        far_slots = jnp.einsum('bck,bkn->bcn', u_slots.reshape(N_LEAF, CAP, K), final_coeffs).astype(jnp.bfloat16)
        far_term = far_slots.reshape(N_LEAF * CAP, col_count)[slot_index]
        x_blocks = x_one.reshape(BPD, BLK, col_count)
        chosen = x_blocks[index_one].astype(jnp.float32)
        keep_mask = (jnp.arange(NEAR, dtype=jnp.int32)[None, :] < count_one[:, None]).astype(jnp.float32)
        weighted = block_weights.astype(jnp.float32) * keep_mask[:, :, None, None]
        near_term = jnp.einsum('gjab,gjbn->gan', weighted, chosen).reshape(ROWS_DEV, col_count)
        return (far_term.astype(jnp.float32) + near_term).astype(jnp.bfloat16)

    result = lax.map(one_device, (x_groups, owner_groups, field_groups, block_groups, index_groups, count_groups))
    return result.reshape(N_LEAF * ROWS_DEV, col_count)
```

```python
import functools

import jax
import jax.numpy as jnp
from jax import lax
from jax.experimental import pallas as pl
from jax.experimental.pallas import tpu as pltpu
from jax.sharding import PartitionSpec as P

F32 = jnp.float32
BF16 = jnp.bfloat16
CHUNKS = 2
COPIES = 4
VMEM_LIMIT = 48 * 1024 * 1024
VMEM = pl.BlockSpec(memory_space=pltpu.VMEM)
SMEM = pl.BlockSpec(memory_space=pltpu.SMEM)
ANY = pl.BlockSpec(memory_space=pl.ANY)


def cost(flops, nbytes):
    return pl.CostEstimate(flops=flops, bytes_accessed=nbytes, transcendentals=0)


def params():
    return pltpu.CompilerParams(vmem_limit_bytes=VMEM_LIMIT)


def swapped(value, axis, mask):
    return lax.ppermute(value, axis, [(i, i ^ mask) for i in range(lax.axis_size(axis))])


def compress_kernel(first, chunks, me_ref, owner_ref, basis_hbm, fields_hbm, *rest):
    outs, (basis_ref, fields_ref, sems) = rest[:chunks], rest[chunks:]
    rows = basis_ref.shape[0] // COPIES
    copies = []
    for k, (source, target) in enumerate(((basis_hbm, basis_ref), (fields_hbm, fields_ref))):
        for p in range(COPIES):
            part = pl.ds(p * rows, rows)
            copies.append(
                pltpu.make_async_copy(source.at[part], target.at[part], sems.at[k * COPIES + p])
            )
    for copy in copies:
        copy.start()
    relative = owner_ref[...] ^ me_ref[0]
    for copy in copies:
        copy.wait()
    basis_t = basis_ref[...].T
    fields = fields_ref[...]
    width = fields.shape[1] // chunks
    for i in range(outs[0].shape[0]):
        masked = jnp.where(relative == first + 2 * i, basis_t, jnp.zeros((), BF16))
        block = jnp.dot(masked, fields, preferred_element_type=F32)
        for c in range(chunks):
            outs[c][i] = block[:, c * width : (c + 1) * width].astype(outs[c].dtype)


def compress(me, owner_row, basis, fields, first, count, dtype, chunks):
    rows, cols = fields.shape
    width = basis.shape[1]
    return pl.pallas_call(
        functools.partial(compress_kernel, first, chunks),
        out_shape=[jax.ShapeDtypeStruct((count, width, cols // chunks), dtype)] * chunks,
        in_specs=[SMEM, VMEM, ANY, ANY],
        out_specs=[VMEM] * chunks,
        scratch_shapes=[
            pltpu.VMEM((rows, width), BF16),
            pltpu.VMEM((rows, cols), BF16),
            pltpu.SemaphoreType.DMA((2 * COPIES,)),
        ],
        compiler_params=params(),
        cost_estimate=cost(2 * count * rows * cols * width, 4 * rows * cols),
    )(me, owner_row, basis, fields)


def near_kernel(index_ref, count_ref, blocks_ref, fields_ref, near_ref):
    g = pl.program_id(0)
    slots, size = blocks_ref.shape[1:3]
    chosen = []
    for j in range(slots):
        start = pl.multiple_of(index_ref[g, j] * size, size)
        piece = fields_ref[pl.ds(start, size), :]
        chosen.append(jnp.where(j < count_ref[g], piece, jnp.zeros_like(piece)))
    weights = jnp.concatenate([blocks_ref[0, j] for j in range(slots)], axis=1)
    near_ref[...] = jnp.dot(
        weights, jnp.concatenate(chosen, axis=0), preferred_element_type=F32
    )


def near_field(near_index, near_count, near_blocks, fields):
    rows, cols = fields.shape
    blocks, slots, size, _ = near_blocks.shape
    return pl.pallas_call(
        near_kernel,
        out_shape=jax.ShapeDtypeStruct((rows, cols), F32),
        grid_spec=pltpu.PrefetchScalarGridSpec(
            num_scalar_prefetch=2,
            grid=(blocks,),
            in_specs=[
                pl.BlockSpec((1, slots, size, size), lambda g, *_: (g, 0, 0, 0)),
                pl.BlockSpec((rows, cols), lambda g, *_: (0, 0)),
            ],
            out_specs=pl.BlockSpec((size, cols), lambda g, *_: (g, 0)),
        ),
        compiler_params=params(),
        cost_estimate=cost(2 * blocks * slots * size * size * cols, near_blocks.size * 2),
    )(near_index, near_count, near_blocks, fields)


def first_level_kernel(me_ref, rows_ref, own_ref, other_ref, out_ref):
    n = rows_ref.shape[0]
    weights = jnp.concatenate([rows_ref[a ^ me_ref[0]] for a in range(n)], axis=0)
    stacked = jnp.concatenate([own_ref[...], other_ref[...]], axis=0)
    out_ref[...] = jnp.dot(weights, stacked, preferred_element_type=F32).astype(BF16)


def first_level(rhs_me, rows, own, other):
    return pl.pallas_call(
        first_level_kernel,
        out_shape=jax.ShapeDtypeStruct(own.shape, BF16),
        in_specs=[SMEM, VMEM, VMEM, VMEM],
        out_specs=VMEM,
        compiler_params=params(),
        cost_estimate=cost(2 * rows.size * own.shape[1], 2 * rows.size),
    )(rhs_me, rows, own, other)


def later_levels_kernel(me_ref, rows_ref, *rest):
    blocks, out_ref = [ref[...] for ref in rest[:-1]], rest[-1]
    n, count, levels = rows_ref.shape[:3]
    for level in range(levels):
        fresh = []
        for s in range(count):
            weights = jnp.concatenate([rows_ref[a ^ me_ref[0], s, level] for a in range(n)], axis=0)
            stacked = jnp.concatenate([blocks[s], blocks[s ^ (1 << level)]], axis=0)
            fresh.append(jnp.dot(weights, stacked, preferred_element_type=F32).astype(BF16))
        blocks = fresh
    for s in range(count):
        out_ref[s] = blocks[s]


def later_levels(rhs_me, rows, blocks):
    return pl.pallas_call(
        later_levels_kernel,
        out_shape=jax.ShapeDtypeStruct((len(blocks),) + blocks[0].shape, BF16),
        in_specs=[SMEM] + [VMEM] * (1 + len(blocks)),
        out_specs=VMEM,
        compiler_params=params(),
        cost_estimate=cost(2 * rows.size * blocks[0].shape[1], 2 * rows.size),
    )(rhs_me, rows, *blocks)


def far_kernel(first, last, me_ref, owner_ref, basis_ref, blocks_ref, base_ref, *rest):
    out_ref = rest[-1]
    relative = owner_ref[...] ^ me_ref[0]
    basis = basis_ref[...]
    count, width, part_cols = blocks_ref.shape
    masked = [
        jnp.where(relative == first + 2 * i, basis, jnp.zeros((), BF16)) for i in range(count)
    ]
    total = jnp.dot(
        jnp.concatenate(masked, axis=1),
        blocks_ref[...].reshape(count * width, part_cols),
        preferred_element_type=F32,
    )
    total = total.astype(BF16).astype(F32) + base_ref[...]
    if last:
        earlier = [ref[...] for ref in rest[:-1]]
        out_ref[...] = jnp.concatenate(earlier + [total.astype(out_ref.dtype)], axis=1)
    else:
        out_ref[...] = total.astype(out_ref.dtype)


def far_field(me, owner, basis, blocks, base, base_column, first, dtype, earlier=()):
    rows, width = basis.shape
    count, _, part_cols = blocks.shape
    tile = min(rows, 512)
    out_cols = part_cols * (1 + len(earlier))
    part = pl.BlockSpec((tile, part_cols), lambda r: (r, 0))
    return pl.pallas_call(
        functools.partial(far_kernel, first, bool(earlier)),
        out_shape=jax.ShapeDtypeStruct((rows, out_cols), dtype),
        grid=(rows // tile,),
        in_specs=[
            SMEM,
            pl.BlockSpec((tile, 1), lambda r: (r, 0)),
            pl.BlockSpec((tile, width), lambda r: (r, 0)),
            pl.BlockSpec((count, width, part_cols), lambda r: (0, 0, 0)),
            pl.BlockSpec((tile, part_cols), lambda r: (r, base_column)),
        ]
        + [part] * len(earlier),
        out_specs=pl.BlockSpec((tile, out_cols), lambda r: (r, 0)),
        compiler_params=params(),
        cost_estimate=cost(
            2 * count * rows * width * part_cols, rows * (width * 2 + part_cols * 6)
        ),
    )(me, owner, basis, blocks, base, *earlier)


def gathered_rows(value, axis):
    pieces = value[None]
    mask = 1
    order = [0]
    masks = []
    while mask < lax.axis_size(axis):
        masks.append(mask)
        mask *= 2
    for mask in reversed(masks):
        pieces = jnp.concatenate([pieces, swapped(pieces, axis, mask)], axis=0)
        order = order + [o ^ mask for o in order]
    return pieces, order


def in_order(pieces, order):
    return jnp.stack([pieces[order.index(o)] for o in range(len(order))])


def on_device(
    fields, owner, source_basis, field_basis, transfer, near_blocks, near_index, near_count
):
    n_leaf = lax.axis_size("leaf")
    rows, cols = fields.shape
    levels = transfer.shape[1]
    group = 2**levels
    outer = n_leaf // group
    upper = group // 2
    chunks = CHUNKS
    me = lax.axis_index("leaf").astype(jnp.int32)[None]
    rhs_me = lax.axis_index("rhs").astype(jnp.int32)[None]
    owner_row = owner.reshape(1, rows)

    send = list(compress(me, owner_row, source_basis, fields, 1, n_leaf // 2, BF16, chunks))
    got = [swapped(s, "leaf", 1) for s in send]

    transfer, send[0] = lax.optimization_barrier((transfer, send[0]))
    first, order = gathered_rows(transfer[0, 0], "rhs")
    first = in_order(first, order)
    later = transfer[:, 1:]
    spots = [0]
    mask = upper // 2
    while mask:
        later = jnp.concatenate([later, swapped(later, "leaf", 2 * mask)], axis=0)
        spots = spots + [s ^ mask for s in spots]
        mask //= 2
    later, order = gathered_rows(later, "rhs")
    later = jnp.stack(
        [jnp.stack([later[order.index(o), spots.index(s)] for s in range(upper)]) for o in range(len(order))]
    )

    keep = compress(me, owner_row, source_basis, fields, 0, n_leaf // 2, F32, chunks)
    near = near_field(near_index, near_count, near_blocks, fields)
    got[0], near = lax.optimization_barrier((got[0], near))

    bases, others = [], []
    for c in range(chunks):
        total = keep[c] + got[c].astype(F32)
        mine = total[:upper]
        for o in range(1, outer):
            part = total[o * upper : (o + 1) * upper].astype(BF16)
            mine = mine + swapped(part, "leaf", o * group).astype(F32)
        coefficients = mine[0]
        for s in range(1, upper):
            coefficients = coefficients + swapped(mine[s].astype(BF16), "leaf", 2 * s).astype(F32)
        coefficients = coefficients.astype(BF16)
        coefficients = first_level(rhs_me, first, coefficients, swapped(coefficients, "leaf", 1))
        blocks = [coefficients] + [swapped(coefficients, "leaf", 2 * s) for s in range(1, upper)]
        own = later_levels(rhs_me, later, blocks)
        if outer > 1:
            own = jnp.concatenate([own] + [swapped(own, "leaf", o * group) for o in range(1, outer)])
        others.append(swapped(own, "leaf", 1))
        bases.append(far_field(me, owner, field_basis, own, near, c, 0, F32))
    done = []
    for c in range(chunks):
        earlier = done if c == chunks - 1 else ()
        done.append(far_field(me, owner, field_basis, others[c], bases[c], 0, 1, BF16, earlier))
    return done[-1]


def solution(mesh):
    in_specs = (
        P("leaf", "rhs"),
        P("leaf", None),
        P("leaf", None),
        P("leaf", None),
        P("leaf", None, "rhs", None),
        P("leaf", None, None, None),
        P("leaf", None),
        P("leaf"),
    )
    out_specs = P("leaf", "rhs")
    return jax.shard_map(
        on_device, mesh=mesh, in_specs=in_specs, out_specs=out_specs, check_vma=False
    )
```

```python
import functools

import jax
import jax.numpy as jnp
from jax import lax
from jax.experimental import pallas as pl
from jax.experimental.pallas import tpu as pltpu
from jax.sharding import PartitionSpec as P

F32 = jnp.float32
BF16 = jnp.bfloat16
CHUNKS = 2
COPIES = 2
VMEM_LIMIT = 48 * 1024 * 1024
VMEM = pl.BlockSpec(memory_space=pltpu.VMEM)
SMEM = pl.BlockSpec(memory_space=pltpu.SMEM)
HBM = pl.BlockSpec(memory_space=pltpu.HBM)


def cost(microseconds=0):
    return pl.CostEstimate(
        flops=microseconds * 10**9 + 1024, bytes_accessed=1024, transcendentals=0
    )


def params():
    return pltpu.CompilerParams(vmem_limit_bytes=VMEM_LIMIT)


def tie(*values):
    return lax.optimization_barrier(values)


def swapped(value, axis, mask):
    return lax.ppermute(value, axis, [(i, i ^ mask) for i in range(lax.axis_size(axis))])


def compress_kernel(groups, me_ref, owner_hbm, basis_hbm, fields_hbm, *rest):
    outs, (owner_ref, basis_ref, fields_ref, sems) = rest[: len(groups)], rest[len(groups) :]
    rows = basis_ref.shape[0] // COPIES
    copies = [pltpu.make_async_copy(owner_hbm, owner_ref, sems.at[2 * COPIES])]
    for k, (source, target) in enumerate(((basis_hbm, basis_ref), (fields_hbm, fields_ref))):
        for p in range(COPIES):
            part = pl.ds(p * rows, rows)
            copies.append(
                pltpu.make_async_copy(source.at[part], target.at[part], sems.at[k * COPIES + p])
            )
    for copy in copies:
        copy.start()
    for copy in copies[: COPIES + 1]:
        copy.wait()
    relative = owner_ref[...] ^ me_ref[0]
    basis_t = basis_ref[...].T
    for copy in copies[COPIES + 1 :]:
        copy.wait()
    fields = fields_ref[...]
    for out, group in zip(outs, groups):
        for i, j in enumerate(group):
            masked = jnp.where(relative == j, basis_t, jnp.zeros((), BF16))
            out[i] = jnp.dot(masked, fields, preferred_element_type=F32).astype(out.dtype)


def compress(me, owner_row, basis, fields, groups, dtype):
    rows, cols = fields.shape
    width = basis.shape[1]
    count = sum(len(g) for g in groups)
    return list(
        pl.pallas_call(
            functools.partial(compress_kernel, groups),
            out_shape=[jax.ShapeDtypeStruct((len(g), width, cols), dtype) for g in groups],
            in_specs=[SMEM, HBM, HBM, HBM],
            out_specs=[VMEM] * len(groups),
            scratch_shapes=[
                pltpu.VMEM((1, rows), jnp.int32),
                pltpu.VMEM((rows, width), BF16),
                pltpu.VMEM((rows, cols), BF16),
                pltpu.SemaphoreType.DMA((2 * COPIES + 1,)),
            ],
            cost_estimate=cost(2),
        )(me, owner_row, basis, fields)
    )


def near_kernel(index_ref, count_ref, blocks_hbm, fields_ref, near_ref, blocks_ref, sems):
    groups, slots, size, _ = blocks_ref.shape
    copies = [
        pltpu.make_async_copy(blocks_hbm.at[g], blocks_ref.at[g], sems.at[g]) for g in range(groups)
    ]
    for copy in copies:
        copy.start()
    for g, copy in enumerate(copies):
        chosen = []
        for j in range(slots):
            start = pl.multiple_of(index_ref[g, j] * size, size)
            piece = fields_ref[pl.ds(start, size), :]
            chosen.append(jnp.where(j < count_ref[g], piece, jnp.zeros_like(piece)))
        copy.wait()
        weights = jnp.concatenate([blocks_ref[g, j] for j in range(slots)], axis=1)
        near_ref[g * size : (g + 1) * size, :] = jnp.dot(
            weights, jnp.concatenate(chosen, axis=0), preferred_element_type=F32
        )


def near_field(near_index, near_count, near_blocks, fields):
    rows, cols = fields.shape
    return pl.pallas_call(
        near_kernel,
        out_shape=jax.ShapeDtypeStruct((rows, cols), F32),
        in_specs=[SMEM, SMEM, HBM, VMEM],
        out_specs=VMEM,
        scratch_shapes=[
            pltpu.VMEM(near_blocks.shape, BF16),
            pltpu.SemaphoreType.DMA((near_blocks.shape[0],)),
        ],
        compiler_params=params(),
        cost_estimate=cost(6),
    )(near_index, near_count, near_blocks, fields)


def apply_rows(me, pieces, stacked, out):
    product = jnp.dot(jnp.concatenate(pieces, axis=0), stacked, preferred_element_type=F32)
    size = pieces[0].shape[0]
    for o in range(len(pieces)):
        start = pl.multiple_of((me ^ o) * size, size)
        out[pl.ds(start, size), :] = product[o * size : (o + 1) * size].astype(out.dtype)


def first_level_kernel(me_ref, *refs):
    rows, (own_ref, other_ref, out_ref) = refs[:-3], refs[-3:]
    stacked = jnp.concatenate([own_ref[...], other_ref[...]], axis=0)
    apply_rows(me_ref[0], [ref[...] for ref in rows], stacked, out_ref)


def first_level(rhs_me, rows, own, other):
    return pl.pallas_call(
        first_level_kernel,
        out_shape=jax.ShapeDtypeStruct(own.shape, BF16),
        in_specs=[SMEM] + [VMEM] * (len(rows) + 2),
        out_specs=VMEM,
        compiler_params=params(),
        cost_estimate=cost(),
    )(rhs_me, *rows, own, other)


def later_levels_kernel(n_rhs, me_ref, *refs):
    rows, blocks = refs[:n_rhs], refs[n_rhs : -1 - CHUNKS]
    outs, held_ref = refs[-1 - CHUNKS : -1], refs[-1]
    count, levels = rows[0].shape[:2]
    blocks = [ref[...] for ref in blocks]
    for level in range(levels):
        for s in range(count):
            stacked = jnp.concatenate([blocks[s], blocks[s ^ (1 << level)]], axis=0)
            apply_rows(me_ref[0], [ref[s, level] for ref in rows], stacked, held_ref.at[s])
        blocks = [held_ref[s] for s in range(count)]
    width = outs[0].shape[2]
    for s in range(count):
        for c, out in enumerate(outs):
            out[s] = blocks[s][:, c * width : (c + 1) * width]


def later_levels(rhs_me, rows, blocks):
    width, cols = blocks[0].shape
    part = jax.ShapeDtypeStruct((len(blocks), width, cols // CHUNKS), BF16)
    return pl.pallas_call(
        functools.partial(later_levels_kernel, len(rows)),
        out_shape=[part] * CHUNKS,
        in_specs=[SMEM] + [VMEM] * (len(rows) + len(blocks)),
        out_specs=[VMEM] * CHUNKS,
        scratch_shapes=[pltpu.VMEM((len(blocks), width, cols), BF16)],
        compiler_params=params(),
        cost_estimate=cost(),
    )(rhs_me, *rows, *blocks)


def far_tile(me_ref, owner_ref, basis_ref, blocks_ref, base_ref, first, part):
    relative = owner_ref[part, :] ^ me_ref[0]
    basis = basis_ref[part, :]
    count, width, part_cols = blocks_ref.shape
    masked = [
        jnp.where(relative == first + 2 * i, basis, jnp.zeros((), BF16)) for i in range(count)
    ]
    total = jnp.dot(
        jnp.concatenate(masked, axis=1),
        blocks_ref[...].reshape(count * width, part_cols),
        preferred_element_type=F32,
    )
    return total.astype(BF16).astype(F32) + base_ref[part, :]


def far_kernel(first, tile, me_ref, owner_ref, basis_ref, blocks_ref, base_ref, out_ref):
    for t in range(out_ref.shape[0] // tile):
        part = pl.ds(t * tile, tile)
        value = far_tile(me_ref, owner_ref, basis_ref, blocks_ref, base_ref, first, part)
        out_ref[part, :] = value.astype(out_ref.dtype)


def far_field(me, owner, basis, blocks, base, first, dtype):
    rows, width = basis.shape
    count, _, part_cols = blocks.shape
    return pl.pallas_call(
        functools.partial(far_kernel, first, min(rows, 512)),
        out_shape=jax.ShapeDtypeStruct((rows, part_cols), dtype),
        in_specs=[SMEM, VMEM, VMEM, VMEM, VMEM],
        out_specs=VMEM,
        compiler_params=params(),
        cost_estimate=cost(),
    )(me, owner, basis, blocks, base)


def last_kernel(
    first, tile, me_ref, owner_ref, basis_ref, blocks_ref, base_ref, *rest
):
    earlier, (out_hbm, held, sems) = rest[:-3], rest[-3:]
    rows, part_cols = held.shape
    copies = []
    for c, ref in enumerate(earlier):
        target = out_hbm.at[:, pl.ds(c * part_cols, part_cols)]
        copies.append(pltpu.make_async_copy(ref, target, sems.at[c]))
        copies[-1].start()
    for t in range(rows // tile):
        part = pl.ds(t * tile, tile)
        value = far_tile(me_ref, owner_ref, basis_ref, blocks_ref, base_ref, first, part)
        held[part, :] = value.astype(BF16)
        target = out_hbm.at[part, pl.ds(len(earlier) * part_cols, part_cols)]
        copies.append(pltpu.make_async_copy(held.at[part], target, sems.at[len(earlier) + t]))
        copies[-1].start()
    for copy in copies:
        copy.wait()


def last_far_field(me, owner, basis, blocks, base, first, earlier):
    rows, width = basis.shape
    count, _, part_cols = blocks.shape
    tile = min(rows, 512)
    return pl.pallas_call(
        functools.partial(last_kernel, first, tile),
        out_shape=jax.ShapeDtypeStruct((rows, part_cols * (1 + len(earlier))), BF16),
        in_specs=[SMEM] + [VMEM] * (4 + len(earlier)),
        out_specs=HBM,
        scratch_shapes=[
            pltpu.VMEM((rows, part_cols), BF16),
            pltpu.SemaphoreType.DMA((len(earlier) + rows // tile,)),
        ],
        compiler_params=params(),
        cost_estimate=cost(),
    )(me, owner, basis, blocks, base, *earlier)


def on_device(
    fields, owner, source_basis, field_basis, transfer, near_blocks, near_index, near_count
):
    n_leaf = lax.axis_size("leaf")
    rows, cols = fields.shape
    levels = transfer.shape[1]
    group = 2**levels
    outer = n_leaf // group
    upper = group // 2
    chunks = CHUNKS
    n_rhs = lax.axis_size("rhs")
    me = lax.axis_index("leaf").astype(jnp.int32)[None]
    rhs_me = lax.axis_index("rhs").astype(jnp.int32)[None]
    owner_row = owner.reshape(1, rows)

    parts = [list(range(upper - 1, upper // 2 - 1, -1)), list(range(upper // 2 - 1, -1, -1))]

    def groups(low):
        return [[o * group + 2 * s + low for s in part for o in range(outer)] for part in parts]

    send = compress(me, owner_row, source_basis, fields, groups(1), BF16)

    fields, send[0], send[1] = tie(fields, *send)
    got = [swapped(s, "leaf", 1) for s in send]
    keep = compress(me, owner_row, source_basis, fields, groups(0)[:1], F32)

    def reduced(keep, got, part):
        total = keep + got.astype(F32)
        sums = []
        for i in range(len(part)):
            mine = total[i * outer]
            for o in range(1, outer):
                piece = total[i * outer + o].astype(BF16)
                mine = mine + swapped(piece, "leaf", o * group).astype(F32)
            sums.append(mine)
        return sums

    transfer, keep[0] = tie(transfer, keep[0])
    later = {0: transfer[0, 1:]}
    first = {0: transfer[0, 0]}
    later_next = swapped(later[0], "leaf", upper)
    first_next = swapped(first[0], "rhs", n_rhs // 2)

    far_sums = reduced(keep[0], got[0], parts[0])
    arrived = [swapped(v.astype(BF16), "leaf", 2 * s) for s, v in zip(parts[0], far_sums)]
    fields, far_sums[0] = tie(fields, far_sums[0])
    keep += compress(me, owner_row, source_basis, fields, groups(0)[1:], F32)
    near_sums = reduced(keep[1], got[1], parts[1])
    arrived += [swapped(v.astype(BF16), "leaf", 2 * s) for s, v in zip(parts[1][:-1], near_sums)]
    mine = near_sums[-1]

    mine, later_next, first_next = tie(mine, later_next, first_next)
    mask = upper // 2
    while mask:
        later.update({s ^ mask: later_next[i] if later_next.ndim == 4 else later_next for i, s in enumerate(sorted(later))})
        mask //= 2
        if mask:
            later_next = swapped(jnp.stack([later[s] for s in sorted(later)]), "leaf", 2 * mask)
    mask = n_rhs // 2
    while mask:
        first.update({o ^ mask: first_next[i] if first_next.ndim == 3 else first_next for i, o in enumerate(sorted(first))})
        mask //= 2
        if mask:
            first_next = swapped(jnp.stack([first[o] for o in sorted(first)]), "rhs", mask)
    later = {0: jnp.stack([later[s] for s in range(upper)])}
    later_next = swapped(later[0], "rhs", n_rhs // 2)

    coefficients = mine
    for value in arrived:
        coefficients = coefficients + value.astype(F32)
    coefficients = coefficients.astype(BF16)
    coefficients = first_level(
        rhs_me, [first[o] for o in range(n_rhs)], coefficients, swapped(coefficients, "leaf", 1)
    )
    blocks = {s: swapped(coefficients, "leaf", 2 * s) for s in range(upper - 1, 0, -1)}
    blocks[0], later_next, fields = tie(coefficients, later_next, fields)
    mask = n_rhs // 2
    later[mask] = later_next
    mask //= 2
    while mask:
        later.update({o ^ mask: swapped(v, "rhs", mask) for o, v in later.items()})
        mask //= 2
    near = near_field(near_index, near_count, near_blocks, fields)
    near, blocks[0] = tie(near, blocks[0])
    owns = later_levels(rhs_me, [later[o] for o in range(n_rhs)], [blocks[s] for s in range(upper)])
    if outer > 1:
        owns = [
            jnp.concatenate([own] + [swapped(own, "leaf", o * group) for o in range(1, outer)])
            for own in owns
        ]
    others = [swapped(own, "leaf", 1) for own in owns]
    bases = []
    width = cols // chunks
    for c in range(chunks):
        base = near[:, c * width : (c + 1) * width]
        bases.append(far_field(me, owner, field_basis, owns[c], base, 0, F32))
    done = []
    for c in range(chunks - 1):
        done.append(far_field(me, owner, field_basis, others[c], bases[c], 1, BF16))
    return last_far_field(me, owner, field_basis, others[-1], bases[-1], 1, done)


def solution(mesh):
    in_specs = (
        P("leaf", "rhs"),
        P("leaf", None),
        P("leaf", None),
        P("leaf", None),
        P("leaf", None, "rhs", None),
        P("leaf", None, None, None),
        P("leaf", None),
        P("leaf"),
    )
    out_specs = P("leaf", "rhs")
    return jax.shard_map(
        on_device, mesh=mesh, in_specs=in_specs, out_specs=out_specs, check_vma=False
    )
```

```python
import functools

import jax
import jax.numpy as jnp
from jax import lax
from jax.experimental import pallas as pl
from jax.experimental.pallas import tpu as pltpu
from jax.sharding import PartitionSpec as P

F32 = jnp.float32
BF16 = jnp.bfloat16
VMEM_LIMIT = 16 * 1024 * 1024
VMEM = pl.BlockSpec(memory_space=pltpu.VMEM)
SMEM = pl.BlockSpec(memory_space=pltpu.SMEM)
HBM = pl.BlockSpec(memory_space=pltpu.HBM)
ANY = pl.BlockSpec(memory_space=pl.ANY)


def call(kernel, out_shape, values, in_specs, out_spaces, scratch=(), after=()):
    def placed(value, spec):
        space = spec.memory_space
        pinned = space in (pltpu.VMEM, pltpu.HBM)
        return pltpu.with_memory_space_constraint(value, space) if pinned else value

    return pl.pallas_call(
        kernel,
        out_shape=[space(s.shape, s.dtype) for s, space in zip(out_shape, out_spaces)],
        in_specs=list(in_specs) + [ANY if v.ndim > 1 else SMEM for v in after],
        out_specs=[pl.BlockSpec(memory_space=space) for space in out_spaces],
        scratch_shapes=list(scratch),
        compiler_params=pltpu.CompilerParams(vmem_limit_bytes=VMEM_LIMIT),
        cost_estimate=pl.CostEstimate(flops=1024, bytes_accessed=1024, transcendentals=0),
    )(*[placed(v, s) for v, s in zip(values, in_specs)], *after)


def tie(*values):
    return lax.optimization_barrier(values)


def swapped(value, axis, mask):
    return lax.ppermute(value, axis, [(i, i ^ mask) for i in range(lax.axis_size(axis))])


def products(relative, basis_t, fields, groups, outs):
    for out, group in zip(outs, groups):
        for i, j in enumerate(group):
            masked = jnp.where(relative == j, basis_t, jnp.zeros((), BF16))
            out[i] = jnp.dot(masked, fields, preferred_element_type=F32).astype(out.dtype)


def staged_compress_kernel(groups, me_ref, owner_hbm, basis_hbm, fields_hbm, *rest):
    rest = rest[-len(groups) - 4 :]
    outs, (owner_ref, basis_ref, fields_ref, sems) = rest[: len(groups)], rest[len(groups) :]
    pairs = ((owner_hbm, owner_ref), (basis_hbm, basis_ref), (fields_hbm, fields_ref))
    copies = [
        pltpu.make_async_copy(source, target, sems.at[k]) for k, (source, target) in enumerate(pairs)
    ]
    for copy in copies:
        copy.start()
    copies[0].wait()
    relative = owner_ref[...] ^ me_ref[0]
    copies[1].wait()
    basis_t = basis_ref[...].T
    copies[2].wait()
    products(relative, basis_t, fields_ref[...], groups, outs)


def compress_kernel(groups, me_ref, owner_ref, basis_ref, fields_ref, *rest):
    outs = rest[-len(groups) :]
    products(owner_ref[...] ^ me_ref[0], basis_ref[...].T, fields_ref[...], groups, outs)


def compress(me, owner_row, basis, fields, groups, dtype, staged, after=()):
    rows, cols = fields.shape
    width = basis.shape[1]
    held = [
        pltpu.VMEM((1, rows), jnp.int32),
        pltpu.VMEM((rows, width), BF16),
        pltpu.VMEM((rows, cols), BF16),
        pltpu.SemaphoreType.DMA((3,)),
    ]
    return list(
        call(
            functools.partial(staged_compress_kernel if staged else compress_kernel, groups),
            [jax.ShapeDtypeStruct((len(g), width, cols), dtype) for g in groups],
            (me, owner_row, basis, fields),
            [SMEM] + [HBM if staged else VMEM] * 3,
            [pltpu.VMEM] * len(groups),
            held if staged else (),
            after,
        )
    )


def near_kernel(first, index_ref, count_ref, blocks_hbm, fields_ref, *rest):
    near_ref, blocks_ref, sems = rest[-3:]
    groups, slots, size, _ = blocks_ref.shape
    copies = [
        pltpu.make_async_copy(blocks_hbm.at[first + g], blocks_ref.at[g], sems.at[g])
        for g in range(groups)
    ]
    for copy in copies:
        copy.start()
    for g, copy in enumerate(copies):
        chosen = []
        for j in range(slots):
            start = pl.multiple_of(index_ref[first + g, j] * size, size)
            piece = fields_ref[pl.ds(start, size), :]
            live = j < count_ref[first + g]
            chosen.append(jnp.where(live, piece, jnp.zeros_like(piece)))
        copy.wait()
        weights = jnp.concatenate([blocks_ref[g, j] for j in range(slots)], axis=1)
        near_ref[g * size : (g + 1) * size, :] = jnp.dot(
            weights, jnp.concatenate(chosen, axis=0), preferred_element_type=F32
        )


def near_field(near_index, near_count, near_blocks, fields, first, groups, after):
    _, slots, size, _ = near_blocks.shape
    (near,) = call(
        functools.partial(near_kernel, first),
        [jax.ShapeDtypeStruct((groups * size, fields.shape[1]), F32)],
        (near_index, near_count, near_blocks, fields),
        [SMEM, SMEM, HBM, VMEM],
        [pltpu.VMEM],
        [pltpu.VMEM((groups, slots, size, size), BF16), pltpu.SemaphoreType.DMA((groups,))],
        after,
    )
    return near


def apply_rows(me, pieces, stacked, out):
    product = jnp.dot(jnp.concatenate(pieces, axis=0), stacked, preferred_element_type=F32)
    size = pieces[0].shape[0]
    for o in range(len(pieces)):
        start = pl.multiple_of((me ^ o) * size, size)
        out[pl.ds(start, size), :] = product[o * size : (o + 1) * size].astype(out.dtype)


def level_kernel(n_rhs, n_out, level, me_ref, *refs):
    rows, (own_ref, other_ref), outs = refs[: n_rhs * n_out], refs[-2 - n_out : -n_out], refs[-n_out:]
    own, other = own_ref[...], other_ref[...]
    for k, out in enumerate(outs):
        pieces = [ref[level] if k == 0 else ref[...] for ref in rows[k * n_rhs :][:n_rhs]]
        stacked = jnp.concatenate([other, own] if k else [own, other], axis=0)
        apply_rows(me_ref[0], pieces, stacked, out)


def next_level(rhs_me, level, rows, own, other, other_rows=()):
    n_out = 2 if other_rows else 1
    return call(
        functools.partial(level_kernel, len(rows), n_out, level),
        [jax.ShapeDtypeStruct(own.shape, BF16)] * n_out,
        (rhs_me, *rows, *other_rows, own, other),
        [SMEM] + [VMEM] * (len(rows) * n_out + 2),
        [pltpu.VMEM] * n_out,
    )


def far_tile(ids, me_ref, owner_ref, basis_ref, bases, blocks, start, tile):
    part = pl.ds(start, tile)
    rows = bases[0].shape[0]
    base = bases[start // rows][pl.ds(start % rows, tile), :]
    relative = owner_ref[part, :] ^ me_ref[0]
    basis = basis_ref[part, :]
    masked = [jnp.where(relative == j, basis, jnp.zeros((), BF16)) for j in ids]
    stacked = [ref[...] for ref in blocks]
    total = jnp.dot(
        jnp.concatenate(masked, axis=1),
        jnp.concatenate(stacked, axis=0),
        preferred_element_type=F32,
    )
    return total.astype(BF16).astype(F32) + base


def far_kernel(ids, tile, n_base, me_ref, owner_ref, basis_ref, *refs):
    bases, blocks, out_ref = refs[:n_base], refs[n_base:-1], refs[-1]
    for start in range(0, out_ref.shape[0], tile):
        value = far_tile(ids, me_ref, owner_ref, basis_ref, bases, blocks, start, tile)
        out_ref[pl.ds(start, tile), :] = value


def last_far_kernel(ids, tile, n_base, me_ref, owner_ref, basis_ref, *refs):
    bases, blocks, (out_hbm, held_ref, sems) = refs[:n_base], refs[n_base:-3], refs[-3:]
    copies = []
    for t in range(out_hbm.shape[0] // tile):
        value = far_tile(ids, me_ref, owner_ref, basis_ref, bases, blocks, t * tile, tile)
        part = pl.ds(t * tile, tile)
        held_ref[part, :] = value.astype(BF16)
        copies.append(pltpu.make_async_copy(held_ref.at[part], out_hbm.at[part], sems.at[t]))
        copies[-1].start()
    for copy in copies:
        copy.wait()


def far_field(ids, me, owner, basis, bases, blocks, last=False):
    rows, cols = basis.shape[0], bases[0].shape[1]
    tile = min(bases[0].shape[0], 512)
    held = [pltpu.VMEM((rows, cols), BF16), pltpu.SemaphoreType.DMA((rows // tile,))]
    (out,) = call(
        functools.partial(last_far_kernel if last else far_kernel, ids, tile, len(bases)),
        [jax.ShapeDtypeStruct((rows, cols), BF16 if last else F32)],
        (me, owner, basis, *bases, *blocks),
        [SMEM] + [VMEM] * (2 + len(bases) + len(blocks)),
        [pltpu.HBM if last else pltpu.VMEM],
        held if last else (),
    )
    return out


def across(pieces, mask):
    while mask:
        pieces = pieces | {o ^ mask: swapped(v, "rhs", mask) for o, v in pieces.items()}
        mask //= 2
    return pieces


def on_device(
    fields, owner, source_basis, field_basis, transfer, near_blocks, near_index, near_count
):
    n_leaf = lax.axis_size("leaf")
    rows, cols = fields.shape
    levels = transfer.shape[1]
    group = 2**levels
    outer = n_leaf // group
    upper = group // 2
    n_rhs = lax.axis_size("rhs")
    me = lax.axis_index("leaf").astype(jnp.int32)[None]
    rhs_me = lax.axis_index("rhs").astype(jnp.int32)[None]
    owner_row = owner.reshape(1, rows)

    parts = [list(range(upper - 1, 0, -1)), [0]]

    def groups(low):
        return [[o * group + 2 * s + low for s in part for o in range(outer)] for part in parts]

    send = compress(me, owner_row, source_basis, fields, groups(1), BF16, True, [rhs_me])

    fields, send[0], send[1] = tie(fields, *send)
    got = [swapped(s, "leaf", 1) for s in send]
    keep = compress(me, owner_row, source_basis, fields, groups(0)[:1], F32, False)

    def reduced(keep, got, part):
        total = keep + got.astype(F32)
        sums = []
        for i in range(len(part)):
            mine = total[i * outer]
            for o in range(1, outer):
                piece = total[i * outer + o].astype(BF16)
                mine = mine + swapped(piece, "leaf", o * group).astype(F32)
            sums.append(mine)
        return sums

    transfer, keep[0] = tie(transfer, keep[0])
    top = group // 2
    far_rhs = n_rhs // 2
    mine_rows = {0: transfer[0]}
    mine_rows[far_rhs] = swapped(mine_rows[0], "rhs", far_rhs)
    their_rows = {0: swapped(transfer[0, -1], "leaf", top)}
    got[0], mine_rows[far_rhs], their_rows[0] = tie(got[0], mine_rows[far_rhs], their_rows[0])

    sums = [v.astype(BF16) for v in reduced(keep[0], got[0], parts[0])]
    arrived = [swapped(v, "leaf", 2 * s) for s, v in zip(parts[0], sums)]
    keep += compress(me, owner_row, source_basis, fields, groups(0)[1:], F32, False, sums[:1])
    (total,) = reduced(keep[1], got[1], parts[1])
    half = near_blocks.shape[0] // 2
    near = [near_field(near_index, near_count, near_blocks, fields, 0, half, sums[:1])]
    mine_rows = across(mine_rows, far_rhs // 2)
    order = sorted(mine_rows)
    total, near[0] = tie(total, near[0])

    for value in arrived:
        total = total + value.astype(F32)
    coefficients = total.astype(BF16)
    for level in range(levels - 1):
        other = swapped(coefficients, "leaf", 2**level)
        if level == 0:
            their_rows[far_rhs] = swapped(their_rows[0], "rhs", far_rhs)
            coefficients, their_rows[far_rhs] = tie(coefficients, their_rows[far_rhs])
        if level == 1:
            their_rows = across(their_rows, far_rhs // 2)
            coefficients, *values = tie(coefficients, *[their_rows[o] for o in order])
            their_rows = dict(zip(order, values))
        rows = [mine_rows[o] for o in order]
        (coefficients,) = next_level(rhs_me, level, rows, coefficients, other)
    other = swapped(coefficients, "leaf", top)
    near.append(near_field(near_index, near_count, near_blocks, fields, half, half, [coefficients]))
    near[1], coefficients = tie(near[1], coefficients)
    rows = [mine_rows[o] for o in order]
    own = next_level(
        rhs_me, levels - 1, rows, coefficients, other, [their_rows[o] for o in order]
    )

    def add_far(base, known, last=False):
        ids = [o * group + j for j in sorted(known) for o in range(outer)]
        blocks = []
        for j in sorted(known):
            blocks += [known[j]] + [swapped(known[j], "leaf", o * group) for o in range(1, outer)]
        return far_field(ids, me, owner, field_basis, base, blocks, last)

    known = {0: own[0], top: own[1]}
    steps = [1 << k for k in range(levels - 1)]
    total = near
    low, high = steps
    from_low = {j ^ low: swapped(v, "leaf", low) for j, v in known.items()}
    from_high = {j ^ high: swapped(v, "leaf", high) for j, v in known.items()}
    total = [add_far(total, known)]
    total[0], from_high[high], from_low[top ^ low] = tie(
        total[0], from_high[high], from_low[top ^ low]
    )
    rest = {
        low ^ high: swapped(from_high[high], "leaf", low),
        top ^ low ^ high: swapped(from_low[top ^ low], "leaf", high),
    }
    total = [add_far(total, from_low | from_high)]
    return add_far(total, rest, True)


def solution(mesh):
    in_specs = (
        P("leaf", "rhs"),
        P("leaf", None),
        P("leaf", None),
        P("leaf", None),
        P("leaf", None, "rhs", None),
        P("leaf", None, None, None),
        P("leaf", None),
        P("leaf"),
    )
    out_specs = P("leaf", "rhs")
    return jax.shard_map(
        on_device, mesh=mesh, in_specs=in_specs, out_specs=out_specs, check_vma=False
    )
```

```python
import functools

import jax
import jax.numpy as jnp
from jax import lax
from jax.experimental import pallas as pl
from jax.experimental.pallas import tpu as pltpu
from jax.sharding import PartitionSpec as P

F32 = jnp.float32
BF16 = jnp.bfloat16
VMEM_LIMIT = 16 * 1024 * 1024
LANES = 128
VMEM = pl.BlockSpec(memory_space=pltpu.VMEM)
SMEM = pl.BlockSpec(memory_space=pltpu.SMEM)
HBM = pl.BlockSpec(memory_space=pltpu.HBM)
ANY = pl.BlockSpec(memory_space=pl.ANY)


def call(kernel, out_shape, values, in_specs, out_spaces, scratch=(), after=()):
    def placed(value, spec):
        space = spec.memory_space
        pinned = space in (pltpu.VMEM, pltpu.HBM)
        return pltpu.with_memory_space_constraint(value, space) if pinned else value

    return pl.pallas_call(
        kernel,
        out_shape=[space(s.shape, s.dtype) for s, space in zip(out_shape, out_spaces)],
        in_specs=list(in_specs) + [ANY if v.ndim > 1 else SMEM for v in after],
        out_specs=[pl.BlockSpec(memory_space=space) for space in out_spaces],
        scratch_shapes=list(scratch),
        compiler_params=pltpu.CompilerParams(vmem_limit_bytes=VMEM_LIMIT),
        cost_estimate=pl.CostEstimate(flops=1024, bytes_accessed=1024, transcendentals=0),
    )(*[placed(v, s) for v, s in zip(values, in_specs)], *after)


def tie(*values):
    return lax.optimization_barrier(values)


def swapped(value, axis, mask):
    return lax.ppermute(value, axis, [(i, i ^ mask) for i in range(lax.axis_size(axis))])


def products(relative, basis_t, fields, groups, outs):
    for out, group in zip(outs, groups):
        for i, j in enumerate(group):
            masked = jnp.where(relative == j, basis_t, jnp.zeros((), BF16))
            out[i] = jnp.dot(masked, fields, preferred_element_type=F32).astype(out.dtype)


def staged_compress_kernel(groups, me_ref, owner_hbm, basis_hbm, fields_hbm, *rest):
    rest = rest[-len(groups) - 4 :]
    outs, (owner_ref, basis_ref, fields_ref, sems) = rest[: len(groups)], rest[len(groups) :]
    pairs = ((owner_hbm, owner_ref), (basis_hbm, basis_ref), (fields_hbm, fields_ref))
    copies = [
        pltpu.make_async_copy(source, target, sems.at[k]) for k, (source, target) in enumerate(pairs)
    ]
    for copy in copies:
        copy.start()
    copies[0].wait()
    relative = owner_ref[...] ^ me_ref[0]
    copies[1].wait()
    basis_t = basis_ref[...].T
    copies[2].wait()
    products(relative, basis_t, fields_ref[...], groups, outs)


def compress_kernel(groups, me_ref, owner_ref, basis_ref, fields_ref, *rest):
    outs = rest[-len(groups) :]
    products(owner_ref[...] ^ me_ref[0], basis_ref[...].T, fields_ref[...], groups, outs)


def tagged_compress_kernel(groups, me_ref, owner_ref, basis_ref, fields_ref, *rest):
    outs, tag_ref = rest[-len(groups) - 1 : -1], rest[-1]
    relative = owner_ref[...] ^ me_ref[0]
    products(relative, basis_ref[...].T, fields_ref[...], groups, outs)
    wide = jnp.broadcast_to(relative.astype(F32), (LANES, relative.shape[1]))
    tag_ref[...] = wide.T.astype(BF16)


def compress(me, owner_row, basis, fields, groups, dtypes, kind, after=()):
    rows, cols = fields.shape
    width = basis.shape[1]
    staged = kind is staged_compress_kernel
    held = [
        pltpu.VMEM((1, rows), jnp.int32),
        pltpu.VMEM((rows, width), BF16),
        pltpu.VMEM((rows, cols), BF16),
        pltpu.SemaphoreType.DMA((3,)),
    ]
    shapes = [jax.ShapeDtypeStruct((len(g), width, cols), d) for g, d in zip(groups, dtypes)]
    if kind is tagged_compress_kernel:
        shapes.append(jax.ShapeDtypeStruct((rows, LANES), BF16))
    return list(
        call(
            functools.partial(kind, groups),
            shapes,
            (me, owner_row, basis, fields),
            [SMEM] + [HBM if staged else VMEM] * 3,
            [pltpu.VMEM] * len(shapes),
            held if staged else (),
            after,
        )
    )


def near_kernel(first, index_ref, count_ref, blocks_hbm, fields_ref, *rest):
    near_ref, blocks_ref, sems = rest[-3:]
    groups, slots, size, _ = blocks_ref.shape
    copies = [
        pltpu.make_async_copy(blocks_hbm.at[first + g], blocks_ref.at[g], sems.at[g])
        for g in range(groups)
    ]
    for copy in copies:
        copy.start()
    for g, copy in enumerate(copies):
        chosen = []
        for j in range(slots):
            start = pl.multiple_of(index_ref[first + g, j] * size, size)
            piece = fields_ref[pl.ds(start, size), :]
            live = j < count_ref[first + g]
            chosen.append(jnp.where(live, piece, jnp.zeros_like(piece)))
        copy.wait()
        weights = jnp.concatenate([blocks_ref[g, j] for j in range(slots)], axis=1)
        near_ref[g * size : (g + 1) * size, :] = jnp.dot(
            weights, jnp.concatenate(chosen, axis=0), preferred_element_type=F32
        )


def near_field(near_index, near_count, near_blocks, fields, first, groups, after):
    _, slots, size, _ = near_blocks.shape
    (near,) = call(
        functools.partial(near_kernel, first),
        [jax.ShapeDtypeStruct((groups * size, fields.shape[1]), F32)],
        (near_index, near_count, near_blocks, fields),
        [SMEM, SMEM, HBM, VMEM],
        [pltpu.VMEM],
        [pltpu.VMEM((groups, slots, size, size), BF16), pltpu.SemaphoreType.DMA((groups,))],
        after,
    )
    return near


def apply_rows(me, pieces, stacked, out):
    product = jnp.dot(jnp.concatenate(pieces, axis=0), stacked, preferred_element_type=F32)
    size = pieces[0].shape[0]
    for o in range(len(pieces)):
        start = pl.multiple_of((me ^ o) * size, size)
        out[pl.ds(start, size), :] = product[o * size : (o + 1) * size].astype(out.dtype)


def level_kernel(n_rhs, n_out, level, me_ref, *refs):
    rows, (own_ref, other_ref) = refs[: n_rhs * n_out], refs[n_rhs * n_out :][:2]
    outs = refs[-n_out:]
    own, other = own_ref[...], other_ref[...]
    for k, out in enumerate(outs):
        pieces = [ref[level] if k == 0 else ref[...] for ref in rows[k * n_rhs :][:n_rhs]]
        stacked = jnp.concatenate([other, own] if k else [own, other], axis=0)
        apply_rows(me_ref[0], pieces, stacked, out)


def next_level(rhs_me, level, rows, own, other, other_rows=(), after=()):
    n_out = 2 if other_rows else 1
    return call(
        functools.partial(level_kernel, len(rows), n_out, level),
        [jax.ShapeDtypeStruct(own.shape, BF16)] * n_out,
        (rhs_me, *rows, *other_rows, own, other),
        [SMEM] + [VMEM] * (len(rows) * n_out + 2),
        [pltpu.VMEM] * n_out,
        (),
        after,
    )


def far_tile(ids, tag_ref, basis_ref, bases, blocks, start, tile):
    part = pl.ds(start, tile)
    rows = bases[0].shape[0]
    base = bases[start // rows][pl.ds(start % rows, tile), :]
    tag = tag_ref[part, :]
    basis = basis_ref[part, :]
    lanes = [basis[:, k : k + LANES] for k in range(0, basis.shape[1], LANES)]
    masked = [jnp.where(tag == j, piece, jnp.zeros((), BF16)) for j in ids for piece in lanes]
    stacked = [ref[...] for ref in blocks]
    total = jnp.dot(
        jnp.concatenate(masked, axis=1),
        jnp.concatenate(stacked, axis=0),
        preferred_element_type=F32,
    )
    return total.astype(BF16).astype(F32) + base


def far_kernel(ids, tile, n_base, tag_ref, basis_ref, *refs):
    bases, blocks, out_ref = refs[:n_base], refs[n_base:-1], refs[-1]
    for start in range(0, out_ref.shape[0], tile):
        value = far_tile(ids, tag_ref, basis_ref, bases, blocks, start, tile)
        out_ref[pl.ds(start, tile), :] = value


def last_far_kernel(ids, tile, n_base, tag_ref, basis_ref, *refs):
    bases, blocks, (out_hbm, held_ref, sems) = refs[:n_base], refs[n_base:-3], refs[-3:]
    copies = []
    for t in range(out_hbm.shape[0] // tile):
        value = far_tile(ids, tag_ref, basis_ref, bases, blocks, t * tile, tile)
        part = pl.ds(t * tile, tile)
        held_ref[part, :] = value.astype(BF16)
        copies.append(pltpu.make_async_copy(held_ref.at[part], out_hbm.at[part], sems.at[t]))
        copies[-1].start()
    for copy in copies:
        copy.wait()


def far_field(ids, tag, basis, bases, blocks, last=False):
    rows, cols = basis.shape[0], bases[0].shape[1]
    tile = min(bases[0].shape[0], 512)
    held = [pltpu.VMEM((rows, cols), BF16), pltpu.SemaphoreType.DMA((rows // tile,))]
    (out,) = call(
        functools.partial(last_far_kernel if last else far_kernel, ids, tile, len(bases)),
        [jax.ShapeDtypeStruct((rows, cols), BF16 if last else F32)],
        (tag, basis, *bases, *blocks),
        [VMEM] * (2 + len(bases) + len(blocks)),
        [pltpu.HBM if last else pltpu.VMEM],
        held if last else (),
    )
    return out


def across(pieces, mask):
    while mask:
        pieces = pieces | {o ^ mask: swapped(v, "rhs", mask) for o, v in pieces.items()}
        mask //= 2
    return pieces


def on_device(
    fields, owner, source_basis, field_basis, transfer, near_blocks, near_index, near_count
):
    n_leaf = lax.axis_size("leaf")
    rows, cols = fields.shape
    levels = transfer.shape[1]
    group = 2**levels
    outer = n_leaf // group
    upper = group // 2
    n_rhs = lax.axis_size("rhs")
    me = lax.axis_index("leaf").astype(jnp.int32)[None]
    rhs_me = lax.axis_index("rhs").astype(jnp.int32)[None]
    owner_row = owner.reshape(1, rows)

    parts = [list(range(upper - 1, 0, -1)), [0]]

    def groups(low):
        return [[o * group + 2 * s + low for s in part for o in range(outer)] for part in parts]

    odd, even = groups(1), groups(0)
    operands = (me, owner_row, source_basis)
    (send,) = compress(*operands, fields, odd[:1], [BF16], staged_compress_kernel, [rhs_me])
    fields, send = tie(fields, send)
    got = [swapped(send, "leaf", 1)]
    *keep, send = compress(*operands, fields, [even[0], odd[1]], [F32, BF16], compress_kernel)
    got.append(swapped(send, "leaf", 1))

    def reduced(keep, got, part):
        total = keep + got.astype(F32)
        sums = []
        for i in range(len(part)):
            mine = total[i * outer]
            for o in range(1, outer):
                piece = total[i * outer + o].astype(BF16)
                mine = mine + swapped(piece, "leaf", o * group).astype(F32)
            sums.append(mine)
        return sums

    transfer, keep[0] = tie(transfer, keep[0])
    top = group // 2
    far_rhs = n_rhs // 2
    mine_rows = {0: transfer[0]}
    mine_rows[far_rhs] = swapped(mine_rows[0], "rhs", far_rhs)
    their_rows = {0: swapped(transfer[0, -1], "leaf", top)}
    got[0], mine_rows[far_rhs], their_rows[0] = tie(got[0], mine_rows[far_rhs], their_rows[0])

    sums = [v.astype(BF16) for v in reduced(keep[0], got[0], parts[0])]
    arrived = [swapped(v, "leaf", 2 * s) for s, v in zip(parts[0], sums)]
    more, tag = compress(*operands, fields, even[1:], [F32], tagged_compress_kernel, sums[:1])
    keep.append(more)
    (total,) = reduced(keep[1], got[1], parts[1])
    half = near_blocks.shape[0] // 2
    near = [near_field(near_index, near_count, near_blocks, fields, 0, half, sums[:1])]
    mine_rows = across(mine_rows, far_rhs // 2)
    order = sorted(mine_rows)
    total, near[0] = tie(total, near[0])

    for value in arrived:
        total = total + value.astype(F32)
    coefficients = total.astype(BF16)
    for level in range(levels - 1):
        other = swapped(coefficients, "leaf", 2**level)
        if level == 0:
            their_rows[far_rhs] = swapped(their_rows[0], "rhs", far_rhs)
            coefficients, their_rows[far_rhs] = tie(coefficients, their_rows[far_rhs])
        if level == 1:
            their_rows = across(their_rows, far_rhs // 2)
            coefficients, *values = tie(coefficients, *[their_rows[o] for o in order])
            their_rows = dict(zip(order, values))
        rows = [mine_rows[o] for o in order]
        (coefficients,) = next_level(rhs_me, level, rows, coefficients, other)
    other = swapped(coefficients, "leaf", top)
    near.append(near_field(near_index, near_count, near_blocks, fields, half, half, [coefficients]))
    rows, more = [mine_rows[o] for o in order], [their_rows[o] for o in order]
    own = next_level(rhs_me, levels - 1, rows, coefficients, other, more, near[1:])

    def add_far(base, known, last=False):
        ids = [o * group + j for j in sorted(known) for o in range(outer)]
        blocks = []
        for j in sorted(known):
            blocks += [known[j]] + [swapped(known[j], "leaf", o * group) for o in range(1, outer)]
        return far_field(ids, tag, field_basis, base, blocks, last)

    known = {0: own[0], top: own[1]}
    steps = [1 << k for k in range(levels - 1)]
    total = near
    low, high = steps
    from_low = {j ^ low: swapped(v, "leaf", low) for j, v in known.items()}
    from_high = {j ^ high: swapped(v, "leaf", high) for j, v in known.items()}
    total = [add_far(total, known)]
    rest = {
        low ^ high: swapped(from_high[high], "leaf", low),
        top ^ low ^ high: swapped(from_low[top ^ low], "leaf", high),
    }
    total = [add_far(total, from_low | from_high)]
    return add_far(total, rest, True)


def solution(mesh):
    in_specs = (
        P("leaf", "rhs"),
        P("leaf", None),
        P("leaf", None),
        P("leaf", None),
        P("leaf", None, "rhs", None),
        P("leaf", None, None, None),
        P("leaf", None),
        P("leaf"),
    )
    out_specs = P("leaf", "rhs")
    return jax.shard_map(
        on_device, mesh=mesh, in_specs=in_specs, out_specs=out_specs, check_vma=False
    )
```

```python
import functools

import jax
import jax.numpy as jnp
from jax import lax
from jax.experimental import pallas as pl
from jax.experimental.pallas import tpu as pltpu
from jax.sharding import PartitionSpec as P

F32 = jnp.float32
BF16 = jnp.bfloat16
VMEM_LIMIT = 16 * 1024 * 1024
LANES = 128
VMEM = pl.BlockSpec(memory_space=pltpu.VMEM)
SMEM = pl.BlockSpec(memory_space=pltpu.SMEM)
HBM = pl.BlockSpec(memory_space=pltpu.HBM)
ANY = pl.BlockSpec(memory_space=pl.ANY)


def call(kernel, out_shape, values, in_specs, out_spaces, scratch=(), after=()):
    def placed(value, spec):
        space = spec.memory_space
        pinned = space in (pltpu.VMEM, pltpu.HBM)
        return pltpu.with_memory_space_constraint(value, space) if pinned else value

    return pl.pallas_call(
        kernel,
        out_shape=[space(s.shape, s.dtype) for s, space in zip(out_shape, out_spaces)],
        in_specs=list(in_specs) + [ANY if v.ndim > 1 else SMEM for v in after],
        out_specs=[pl.BlockSpec(memory_space=space) for space in out_spaces],
        scratch_shapes=list(scratch),
        compiler_params=pltpu.CompilerParams(vmem_limit_bytes=VMEM_LIMIT),
        cost_estimate=pl.CostEstimate(flops=1024, bytes_accessed=1024, transcendentals=0),
    )(*[placed(v, s) for v, s in zip(values, in_specs)], *after)


def tie(*values):
    return lax.optimization_barrier(values)


def swapped(value, axis, mask):
    return lax.ppermute(value, axis, [(i, i ^ mask) for i in range(lax.axis_size(axis))])


def products(relative, basis_t, fields, groups, outs):
    for out, group in zip(outs, groups):
        for i, j in enumerate(group):
            masked = jnp.where(relative == j, basis_t, jnp.zeros((), BF16))
            out[i] = jnp.dot(masked, fields, preferred_element_type=F32).astype(out.dtype)


def staged_compress_kernel(groups, me_ref, owner_hbm, basis_hbm, fields_hbm, *rest):
    rest = rest[-len(groups) - 4 :]
    outs, (owner_ref, basis_ref, fields_ref, sems) = rest[: len(groups)], rest[len(groups) :]
    pairs = ((owner_hbm, owner_ref), (basis_hbm, basis_ref), (fields_hbm, fields_ref))
    copies = [
        pltpu.make_async_copy(source, target, sems.at[k]) for k, (source, target) in enumerate(pairs)
    ]
    for copy in copies:
        copy.start()
    copies[0].wait()
    relative = owner_ref[...] ^ me_ref[0]
    copies[1].wait()
    basis_t = basis_ref[...].T
    copies[2].wait()
    products(relative, basis_t, fields_ref[...], groups, outs)


def compress_kernel(groups, me_ref, owner_ref, basis_ref, fields_ref, *rest):
    outs = rest[-len(groups) :]
    products(owner_ref[...] ^ me_ref[0], basis_ref[...].T, fields_ref[...], groups, outs)


def tagged_compress_kernel(groups, me_ref, owner_ref, basis_ref, fields_ref, *rest):
    outs, tag_ref = rest[-len(groups) - 1 : -1], rest[-1]
    relative = owner_ref[...] ^ me_ref[0]
    products(relative, basis_ref[...].T, fields_ref[...], groups, outs)
    wide = jnp.broadcast_to(relative.astype(F32), (LANES, relative.shape[1]))
    tag_ref[...] = wide.T.astype(BF16)


def compress(me, owner_row, basis, fields, groups, dtypes, kind, after=()):
    rows, cols = fields.shape
    width = basis.shape[1]
    staged = kind is staged_compress_kernel
    held = [
        pltpu.VMEM((1, rows), jnp.int32),
        pltpu.VMEM((rows, width), BF16),
        pltpu.VMEM((rows, cols), BF16),
        pltpu.SemaphoreType.DMA((3,)),
    ]
    shapes = [jax.ShapeDtypeStruct((len(g), width, cols), d) for g, d in zip(groups, dtypes)]
    if kind is tagged_compress_kernel:
        shapes.append(jax.ShapeDtypeStruct((rows, LANES), BF16))
    return list(
        call(
            functools.partial(kind, groups),
            shapes,
            (me, owner_row, basis, fields),
            [SMEM] + [HBM if staged else VMEM] * 3,
            [pltpu.VMEM] * len(shapes),
            held if staged else (),
            after,
        )
    )


def near_kernel(first, index_ref, count_ref, blocks_hbm, fields_ref, *rest):
    near_ref, blocks_ref, sems = rest[-3:]
    groups, slots, size, _ = blocks_ref.shape
    copies = [
        pltpu.make_async_copy(blocks_hbm.at[first + g], blocks_ref.at[g], sems.at[g])
        for g in range(groups)
    ]
    for copy in copies:
        copy.start()
    for g, copy in enumerate(copies):
        chosen = []
        for j in range(slots):
            start = pl.multiple_of(index_ref[first + g, j] * size, size)
            piece = fields_ref[pl.ds(start, size), :]
            live = j < count_ref[first + g]
            chosen.append(jnp.where(live, piece, jnp.zeros_like(piece)))
        copy.wait()
        weights = jnp.concatenate([blocks_ref[g, j] for j in range(slots)], axis=1)
        near_ref[g * size : (g + 1) * size, :] = jnp.dot(
            weights, jnp.concatenate(chosen, axis=0), preferred_element_type=F32
        )


def near_field(near_index, near_count, near_blocks, fields, first, groups, after):
    _, slots, size, _ = near_blocks.shape
    (near,) = call(
        functools.partial(near_kernel, first),
        [jax.ShapeDtypeStruct((groups * size, fields.shape[1]), F32)],
        (near_index, near_count, near_blocks, fields),
        [SMEM, SMEM, HBM, VMEM],
        [pltpu.VMEM],
        [pltpu.VMEM((groups, slots, size, size), BF16), pltpu.SemaphoreType.DMA((groups,))],
        after,
    )
    return near


def apply_rows(me, pieces, stacked, out):
    product = jnp.dot(jnp.concatenate(pieces, axis=0), stacked, preferred_element_type=F32)
    size = pieces[0].shape[0]
    for o in range(len(pieces)):
        start = pl.multiple_of((me ^ o) * size, size)
        out[pl.ds(start, size), :] = product[o * size : (o + 1) * size].astype(out.dtype)


def first_levels_kernel(n_rhs, me_ref, *refs):
    rows, pair_rows = refs[:n_rhs], refs[n_rhs : 2 * n_rhs]
    own_ref, low_ref, mid_ref, both_ref, out_ref, held_ref = refs[2 * n_rhs :]
    stacked = jnp.concatenate([own_ref[...], low_ref[...]], axis=0)
    apply_rows(me_ref[0], [ref[0] for ref in rows], stacked, held_ref.at[0])
    stacked = jnp.concatenate([mid_ref[...], both_ref[...]], axis=0)
    apply_rows(me_ref[0], [ref[0] for ref in pair_rows], stacked, held_ref.at[1])
    stacked = jnp.concatenate([held_ref[0], held_ref[1]], axis=0)
    apply_rows(me_ref[0], [ref[1] for ref in rows], stacked, out_ref)


def first_levels(rhs_me, rows, pair_rows, values):
    shape = values[0].shape
    (out,) = call(
        functools.partial(first_levels_kernel, len(rows)),
        [jax.ShapeDtypeStruct(shape, BF16)],
        (rhs_me, *rows, *pair_rows, *values),
        [SMEM] + [VMEM] * (2 * len(rows) + len(values)),
        [pltpu.VMEM],
        [pltpu.VMEM((2,) + shape, BF16)],
    )
    return out


def last_level_kernel(n_rhs, me_ref, *refs):
    rows, pair_rows = refs[:n_rhs], refs[n_rhs : 2 * n_rhs]
    own, other = [ref[...] for ref in refs[2 * n_rhs :][:2]]
    level = rows[0].shape[0] - 1
    stacked = jnp.concatenate([own, other], axis=0)
    apply_rows(me_ref[0], [ref[level] for ref in rows], stacked, refs[-2])
    stacked = jnp.concatenate([other, own], axis=0)
    apply_rows(me_ref[0], [ref[1] for ref in pair_rows], stacked, refs[-1])


def last_level(rhs_me, rows, pair_rows, own, other, after):
    return call(
        functools.partial(last_level_kernel, len(rows)),
        [jax.ShapeDtypeStruct(own.shape, BF16)] * 2,
        (rhs_me, *rows, *pair_rows, own, other),
        [SMEM] + [VMEM] * (2 * len(rows) + 2),
        [pltpu.VMEM] * 2,
        (),
        after,
    )


def far_tile(ids, tag_ref, basis_ref, bases, blocks, start, tile):
    part = pl.ds(start, tile)
    rows = bases[0].shape[0]
    base = bases[start // rows][pl.ds(start % rows, tile), :]
    tag = tag_ref[part, :]
    basis = basis_ref[part, :]
    lanes = [basis[:, k : k + LANES] for k in range(0, basis.shape[1], LANES)]
    masked = [jnp.where(tag == j, piece, jnp.zeros((), BF16)) for j in ids for piece in lanes]
    stacked = [ref[...] for ref in blocks]
    total = jnp.dot(
        jnp.concatenate(masked, axis=1),
        jnp.concatenate(stacked, axis=0),
        preferred_element_type=F32,
    )
    return total.astype(BF16).astype(F32) + base


def far_kernel(ids, tile, n_base, tag_ref, basis_ref, *refs):
    bases, blocks, out_ref = refs[:n_base], refs[n_base:-1], refs[-1]
    for start in range(0, out_ref.shape[0], tile):
        value = far_tile(ids, tag_ref, basis_ref, bases, blocks, start, tile)
        out_ref[pl.ds(start, tile), :] = value


def last_far_kernel(ids, tile, n_base, tag_ref, basis_ref, *refs):
    bases, blocks, (out_hbm, held_ref, sems) = refs[:n_base], refs[n_base:-3], refs[-3:]
    copies = []
    for t in range(out_hbm.shape[0] // tile):
        value = far_tile(ids, tag_ref, basis_ref, bases, blocks, t * tile, tile)
        part = pl.ds(t * tile, tile)
        held_ref[part, :] = value.astype(BF16)
        copies.append(pltpu.make_async_copy(held_ref.at[part], out_hbm.at[part], sems.at[t]))
        copies[-1].start()
    for copy in copies:
        copy.wait()


def far_field(ids, tag, basis, bases, blocks, last=False):
    rows, cols = basis.shape[0], bases[0].shape[1]
    tile = min(bases[0].shape[0], 512)
    held = [pltpu.VMEM((rows, cols), BF16), pltpu.SemaphoreType.DMA((rows // tile,))]
    (out,) = call(
        functools.partial(last_far_kernel if last else far_kernel, ids, tile, len(bases)),
        [jax.ShapeDtypeStruct((rows, cols), BF16 if last else F32)],
        (tag, basis, *bases, *blocks),
        [VMEM] * (2 + len(bases) + len(blocks)),
        [pltpu.HBM if last else pltpu.VMEM],
        held if last else (),
    )
    return out


def across(pieces, mask):
    while mask:
        pieces = pieces | {o ^ mask: swapped(v, "rhs", mask) for o, v in pieces.items()}
        mask //= 2
    return pieces


def on_device(
    fields, owner, source_basis, field_basis, transfer, near_blocks, near_index, near_count
):
    n_leaf = lax.axis_size("leaf")
    rows, cols = fields.shape
    levels = transfer.shape[1]
    group = 2**levels
    outer = n_leaf // group
    upper = group // 2
    n_rhs = lax.axis_size("rhs")
    me = lax.axis_index("leaf").astype(jnp.int32)[None]
    rhs_me = lax.axis_index("rhs").astype(jnp.int32)[None]
    owner_row = owner.reshape(1, rows)

    parts = [list(range(upper - 1, upper // 2 - 1, -1)), list(range(upper // 2 - 1, -1, -1))]

    def groups(low):
        return [[o * group + 2 * s + low for s in part for o in range(outer)] for part in parts]

    odd, even = groups(1), groups(0)
    operands = (me, owner_row, source_basis)
    (send,) = compress(*operands, fields, odd[:1], [BF16], staged_compress_kernel, [rhs_me])
    fields, send = tie(fields, send)
    got = [swapped(send, "leaf", 1)]
    *keep, send = compress(*operands, fields, [even[0], odd[1]], [F32, BF16], compress_kernel)
    got.append(swapped(send, "leaf", 1))

    def reduced(keep, got, part):
        total = keep + got.astype(F32)
        sums = []
        for i in range(len(part)):
            mine = total[i * outer]
            for o in range(1, outer):
                piece = total[i * outer + o].astype(BF16)
                mine = mine + swapped(piece, "leaf", o * group).astype(F32)
            sums.append(mine)
        return sums

    transfer, keep[0] = tie(transfer, keep[0])
    low, mid, top = 1, 2, group // 2
    far_rhs = n_rhs // 2
    mine_rows = {0: transfer[0], far_rhs: swapped(transfer[0], "rhs", far_rhs)}
    pair = [swapped(transfer[0, 0], "leaf", mid), swapped(transfer[0, -1], "leaf", top)]

    sums = [v.astype(BF16) for v in reduced(keep[0], got[0], parts[0])]
    arrived = [swapped(v, "leaf", 2 * s) for s, v in zip(parts[0], sums)]
    more, tag = compress(*operands, fields, even[1:], [F32], tagged_compress_kernel, sums[:1])
    got[1], mine_rows[0], mine_rows[far_rhs], *pair = tie(
        got[1], mine_rows[0], mine_rows[far_rhs], *pair
    )
    pair_rows = {0: jnp.stack(pair)}
    pair_rows[far_rhs] = swapped(pair_rows[0], "rhs", far_rhs)
    *near_sums, total = reduced(more, got[1], parts[1])
    for s, v in zip(parts[1], near_sums):
        arrived.append(swapped(v.astype(BF16), "leaf", 2 * s))
    half = near_blocks.shape[0] // 2
    near = [near_field(near_index, near_count, near_blocks, fields, 0, half, sums[:1])]
    mine_rows = across(mine_rows, far_rhs // 2)
    order = sorted(mine_rows)
    total, near[0], pair_rows[far_rhs] = tie(total, near[0], pair_rows[far_rhs])

    for value in arrived[len(sums) :] + arrived[: len(sums)]:
        total = total + value.astype(F32)
    coefficients = total.astype(BF16)
    values = [swapped(coefficients, "leaf", mask) for mask in (low, mid, low ^ mid)]
    pair_rows = across(pair_rows, far_rhs // 2)
    rows, pair_rows = [[r[o] for o in order] for r in (mine_rows, pair_rows)]
    coefficients = first_levels(rhs_me, rows, pair_rows, [coefficients] + values)
    other = swapped(coefficients, "leaf", top)
    near.append(near_field(near_index, near_count, near_blocks, fields, half, half, [coefficients]))
    own = last_level(rhs_me, rows, pair_rows, coefficients, other, near[1:])

    def add_far(base, known, last=False):
        ids = [o * group + j for j in sorted(known) for o in range(outer)]
        blocks = []
        for j in sorted(known):
            blocks += [known[j]] + [swapped(known[j], "leaf", o * group) for o in range(1, outer)]
        return far_field(ids, tag, field_basis, base, blocks, last)

    known = {0: own[0], top: own[1]}
    total = near
    high = mid
    from_low = {j ^ low: swapped(v, "leaf", low) for j, v in known.items()}
    from_high = {j ^ high: swapped(v, "leaf", high) for j, v in known.items()}
    total = [add_far(total, known)]
    rest = {
        low ^ high: swapped(from_high[high], "leaf", low),
        top ^ low ^ high: swapped(from_low[top ^ low], "leaf", high),
    }
    total = [add_far(total, from_low | from_high)]
    return add_far(total, rest, True)


def solution(mesh):
    in_specs = (
        P("leaf", "rhs"),
        P("leaf", None),
        P("leaf", None),
        P("leaf", None),
        P("leaf", None, "rhs", None),
        P("leaf", None, None, None),
        P("leaf", None),
        P("leaf"),
    )
    out_specs = P("leaf", "rhs")
    return jax.shard_map(
        on_device, mesh=mesh, in_specs=in_specs, out_specs=out_specs, check_vma=False
    )
```

```python
import functools

import jax
import jax.numpy as jnp
from jax import lax
from jax.experimental import pallas as pl
from jax.experimental.pallas import tpu as pltpu
from jax.sharding import PartitionSpec as P

F32 = jnp.float32
BF16 = jnp.bfloat16
VMEM_LIMIT = 16 * 1024 * 1024
LANES = 128
VMEM = pl.BlockSpec(memory_space=pltpu.VMEM)
SMEM = pl.BlockSpec(memory_space=pltpu.SMEM)
HBM = pl.BlockSpec(memory_space=pltpu.HBM)
ANY = pl.BlockSpec(memory_space=pl.ANY)


def call(kernel, out_shape, values, in_specs, out_spaces, scratch=(), after=()):
    def placed(value, spec):
        space = spec.memory_space
        pinned = space in (pltpu.VMEM, pltpu.HBM)
        return pltpu.with_memory_space_constraint(value, space) if pinned else value

    return pl.pallas_call(
        kernel,
        out_shape=[space(s.shape, s.dtype) for s, space in zip(out_shape, out_spaces)],
        in_specs=list(in_specs) + [ANY if v.ndim > 1 else SMEM for v in after],
        out_specs=[pl.BlockSpec(memory_space=space) for space in out_spaces],
        scratch_shapes=list(scratch),
        compiler_params=pltpu.CompilerParams(vmem_limit_bytes=VMEM_LIMIT),
        cost_estimate=pl.CostEstimate(flops=1024, bytes_accessed=1024, transcendentals=0),
    )(*[placed(v, s) for v, s in zip(values, in_specs)], *after)


def tie(*values):
    return lax.optimization_barrier(values)


def swapped(value, axis, mask):
    return lax.ppermute(value, axis, [(i, i ^ mask) for i in range(lax.axis_size(axis))])


def products(relative, basis_t, fields, groups, outs):
    for out, group in zip(outs, groups):
        for i, j in enumerate(group):
            masked = jnp.where(relative == j, basis_t, jnp.zeros((), BF16))
            out[i] = jnp.dot(masked, fields, preferred_element_type=F32).astype(out.dtype)


def staged_compress_kernel(groups, me_ref, owner_hbm, basis_hbm, fields_hbm, *rest):
    rest = rest[-len(groups) - 4 :]
    outs, (owner_ref, basis_ref, fields_ref, sems) = rest[: len(groups)], rest[len(groups) :]
    pairs = ((owner_hbm, owner_ref), (basis_hbm, basis_ref), (fields_hbm, fields_ref))
    copies = [
        pltpu.make_async_copy(source, target, sems.at[k]) for k, (source, target) in enumerate(pairs)
    ]
    for copy in copies:
        copy.start()
    copies[0].wait()
    relative = owner_ref[...] ^ me_ref[0]
    copies[1].wait()
    basis_t = basis_ref[...].T
    copies[2].wait()
    products(relative, basis_t, fields_ref[...], groups, outs)


def compress_kernel(groups, me_ref, owner_ref, basis_ref, fields_ref, *rest):
    outs = rest[-len(groups) :]
    products(owner_ref[...] ^ me_ref[0], basis_ref[...].T, fields_ref[...], groups, outs)


def tagged_compress_kernel(groups, me_ref, owner_ref, basis_ref, fields_ref, *rest):
    outs, tag_ref = rest[-len(groups) - 1 : -1], rest[-1]
    relative = owner_ref[...] ^ me_ref[0]
    products(relative, basis_ref[...].T, fields_ref[...], groups, outs)
    wide = jnp.broadcast_to(relative.astype(F32), (LANES, relative.shape[1]))
    tag_ref[...] = wide.T.astype(BF16)


def compress(me, owner_row, basis, fields, groups, dtypes, kind, after=()):
    rows, cols = fields.shape
    width = basis.shape[1]
    staged = kind is staged_compress_kernel
    held = [
        pltpu.VMEM((1, rows), jnp.int32),
        pltpu.VMEM((rows, width), BF16),
        pltpu.VMEM((rows, cols), BF16),
        pltpu.SemaphoreType.DMA((3,)),
    ]
    shapes = [jax.ShapeDtypeStruct((len(g), width, cols), d) for g, d in zip(groups, dtypes)]
    if kind is tagged_compress_kernel:
        shapes.append(jax.ShapeDtypeStruct((rows, LANES), BF16))
    return list(
        call(
            functools.partial(kind, groups),
            shapes,
            (me, owner_row, basis, fields),
            [SMEM] + [HBM if staged else VMEM] * 3,
            [pltpu.VMEM] * len(shapes),
            held if staged else (),
            after,
        )
    )


def near_kernel(first, index_ref, count_ref, blocks_hbm, fields_ref, *rest):
    near_ref, blocks_ref, sems = rest[-3:]
    groups, slots, size, _ = blocks_ref.shape
    copies = [
        pltpu.make_async_copy(blocks_hbm.at[first + g], blocks_ref.at[g], sems.at[g])
        for g in range(groups)
    ]
    for copy in copies:
        copy.start()
    for g, copy in enumerate(copies):
        chosen = []
        for j in range(slots):
            start = pl.multiple_of(index_ref[first + g, j] * size, size)
            piece = fields_ref[pl.ds(start, size), :]
            live = j < count_ref[first + g]
            chosen.append(jnp.where(live, piece, jnp.zeros_like(piece)))
        copy.wait()
        weights = jnp.concatenate([blocks_ref[g, j] for j in range(slots)], axis=1)
        near_ref[g * size : (g + 1) * size, :] = jnp.dot(
            weights, jnp.concatenate(chosen, axis=0), preferred_element_type=F32
        )


def near_field(near_index, near_count, near_blocks, fields, first, groups, after):
    _, slots, size, _ = near_blocks.shape
    (near,) = call(
        functools.partial(near_kernel, first),
        [jax.ShapeDtypeStruct((groups * size, fields.shape[1]), F32)],
        (near_index, near_count, near_blocks, fields),
        [SMEM, SMEM, HBM, VMEM],
        [pltpu.VMEM],
        [pltpu.VMEM((groups, slots, size, size), BF16), pltpu.SemaphoreType.DMA((groups,))],
        after,
    )
    return near


def apply_rows(me, pieces, stacked, out):
    product = jnp.dot(jnp.concatenate(pieces, axis=0), stacked, preferred_element_type=F32)
    size = pieces[0].shape[0]
    for o in range(len(pieces)):
        start = pl.multiple_of((me ^ o) * size, size)
        out[pl.ds(start, size), :] = product[o * size : (o + 1) * size].astype(out.dtype)


def first_levels_kernel(n_rhs, me_ref, *refs):
    rows, pair_rows = refs[:n_rhs], refs[n_rhs : 2 * n_rhs]
    own_ref, low_ref, mid_ref, both_ref, out_ref, held_ref = refs[2 * n_rhs :]
    stacked = jnp.concatenate([own_ref[...], low_ref[...]], axis=0)
    apply_rows(me_ref[0], [ref[0] for ref in rows], stacked, held_ref.at[0])
    stacked = jnp.concatenate([mid_ref[...], both_ref[...]], axis=0)
    apply_rows(me_ref[0], [ref[0] for ref in pair_rows], stacked, held_ref.at[1])
    stacked = jnp.concatenate([held_ref[0], held_ref[1]], axis=0)
    apply_rows(me_ref[0], [ref[1] for ref in rows], stacked, out_ref)


def first_levels(rhs_me, rows, pair_rows, values):
    shape = values[0].shape
    (out,) = call(
        functools.partial(first_levels_kernel, len(rows)),
        [jax.ShapeDtypeStruct(shape, BF16)],
        (rhs_me, *rows, *pair_rows, *values),
        [SMEM] + [VMEM] * (2 * len(rows) + len(values)),
        [pltpu.VMEM],
        [pltpu.VMEM((2,) + shape, BF16)],
    )
    return out


def last_level_kernel(n_rhs, me_ref, *refs):
    rows, pair_rows = refs[:n_rhs], refs[n_rhs : 2 * n_rhs]
    own, other = [ref[...] for ref in refs[2 * n_rhs :][:2]]
    level = rows[0].shape[0] - 1
    stacked = jnp.concatenate([own, other], axis=0)
    apply_rows(me_ref[0], [ref[level] for ref in rows], stacked, refs[-2])
    stacked = jnp.concatenate([other, own], axis=0)
    apply_rows(me_ref[0], [ref[1] for ref in pair_rows], stacked, refs[-1])


def last_level(rhs_me, rows, pair_rows, own, other, after):
    return call(
        functools.partial(last_level_kernel, len(rows)),
        [jax.ShapeDtypeStruct(own.shape, BF16)] * 2,
        (rhs_me, *rows, *pair_rows, own, other),
        [SMEM] + [VMEM] * (2 * len(rows) + 2),
        [pltpu.VMEM] * 2,
        (),
        after,
    )


def far_tile(ids, tag_ref, basis_ref, bases, blocks, start, tile):
    part = pl.ds(start, tile)
    rows = bases[0].shape[0]
    base = bases[start // rows][pl.ds(start % rows, tile), :]
    tag = tag_ref[part, :]
    basis = basis_ref[part, :]
    lanes = [basis[:, k : k + LANES] for k in range(0, basis.shape[1], LANES)]
    masked = [jnp.where(tag == j, piece, jnp.zeros((), BF16)) for j in ids for piece in lanes]
    stacked = [ref[...] for ref in blocks]
    total = jnp.dot(
        jnp.concatenate(masked, axis=1),
        jnp.concatenate(stacked, axis=0),
        preferred_element_type=F32,
    )
    return total.astype(BF16).astype(F32) + base


def far_kernel(ids, tile, n_base, tag_ref, basis_ref, *refs):
    bases, blocks, out_ref = refs[:n_base], refs[n_base:-1], refs[-1]
    for start in range(0, out_ref.shape[0], tile):
        value = far_tile(ids, tag_ref, basis_ref, bases, blocks, start, tile)
        out_ref[pl.ds(start, tile), :] = value


def last_far_kernel(ids, tile, n_base, tag_ref, basis_ref, *refs):
    bases, blocks, (out_hbm, held_ref, sems) = refs[:n_base], refs[n_base:-3], refs[-3:]
    copies = []
    for t in range(out_hbm.shape[0] // tile):
        value = far_tile(ids, tag_ref, basis_ref, bases, blocks, t * tile, tile)
        part = pl.ds(t * tile, tile)
        held_ref[part, :] = value.astype(BF16)
        copies.append(pltpu.make_async_copy(held_ref.at[part], out_hbm.at[part], sems.at[t]))
        copies[-1].start()
    for copy in copies:
        copy.wait()


def far_field(ids, tag, basis, bases, blocks, last=False):
    rows, cols = basis.shape[0], bases[0].shape[1]
    tile = min(bases[0].shape[0], 512)
    held = [pltpu.VMEM((rows, cols), BF16), pltpu.SemaphoreType.DMA((rows // tile,))]
    (out,) = call(
        functools.partial(last_far_kernel if last else far_kernel, ids, tile, len(bases)),
        [jax.ShapeDtypeStruct((rows, cols), BF16 if last else F32)],
        (tag, basis, *bases, *blocks),
        [VMEM] * (2 + len(bases) + len(blocks)),
        [pltpu.HBM if last else pltpu.VMEM],
        held if last else (),
    )
    return out


def across(pieces, mask):
    while mask:
        pieces = pieces | {o ^ mask: swapped(v, "rhs", mask) for o, v in pieces.items()}
        mask //= 2
    return pieces


def on_device(
    fields, owner, source_basis, field_basis, transfer, near_blocks, near_index, near_count
):
    n_leaf = lax.axis_size("leaf")
    rows, cols = fields.shape
    levels = transfer.shape[1]
    group = 2**levels
    outer = n_leaf // group
    upper = group // 2
    n_rhs = lax.axis_size("rhs")
    me = lax.axis_index("leaf").astype(jnp.int32)[None]
    rhs_me = lax.axis_index("rhs").astype(jnp.int32)[None]
    owner_row = owner.reshape(1, rows)

    parts = [list(range(upper - 1, upper // 2 - 1, -1)), list(range(upper // 2 - 1, -1, -1))]

    def groups(low):
        return [[o * group + 2 * s + low for s in part for o in range(outer)] for part in parts]

    odd, even = groups(1), groups(0)
    operands = (me, owner_row, source_basis)
    (send,) = compress(*operands, fields, odd[:1], [BF16], staged_compress_kernel, [rhs_me])
    fields, send = tie(fields, send)
    got = [swapped(send, "leaf", 1)]
    *keep, send = compress(*operands, fields, [even[0], odd[1]], [F32, BF16], compress_kernel)
    got.append(swapped(send, "leaf", 1))

    def reduced(keep, got, part):
        total = keep + got.astype(F32)
        sums = []
        for i in range(len(part)):
            mine = total[i * outer]
            for o in range(1, outer):
                piece = total[i * outer + o].astype(BF16)
                mine = mine + swapped(piece, "leaf", o * group).astype(F32)
            sums.append(mine)
        return sums

    transfer, keep[0] = tie(transfer, keep[0])
    low, mid, top = 1, 2, group // 2
    far_rhs = n_rhs // 2
    mine_rows = {0: transfer[0], far_rhs: swapped(transfer[0], "rhs", far_rhs)}
    pair = [swapped(transfer[0, 0], "leaf", mid), swapped(transfer[0, -1], "leaf", top)]

    sums = [v.astype(BF16) for v in reduced(keep[0], got[0], parts[0])]
    arrived = [swapped(v, "leaf", 2 * s) for s, v in zip(parts[0], sums)]
    more, tag = compress(*operands, fields, even[1:], [F32], tagged_compress_kernel, sums[:1])
    got[1], mine_rows[0], mine_rows[far_rhs], *pair = tie(
        got[1], mine_rows[0], mine_rows[far_rhs], *pair
    )
    pair_rows = {0: jnp.stack(pair)}
    pair_rows[far_rhs] = swapped(pair_rows[0], "rhs", far_rhs)
    *near_sums, total = reduced(more, got[1], parts[1])
    for s, v in zip(parts[1], near_sums):
        arrived.append(swapped(v.astype(BF16), "leaf", 2 * s))
    half = near_blocks.shape[0] // 2
    near = [near_field(near_index, near_count, near_blocks, fields, 0, half, sums[:1])]
    mine_rows = across(mine_rows, far_rhs // 2)
    order = sorted(mine_rows)
    total, near[0], pair_rows[far_rhs] = tie(total, near[0], pair_rows[far_rhs])

    for value in arrived[len(sums) :] + arrived[: len(sums)]:
        total = total + value.astype(F32)
    coefficients = total.astype(BF16)
    values = [swapped(coefficients, "leaf", mask) for mask in (low, mid, low ^ mid)]
    pair_rows = across(pair_rows, far_rhs // 2)
    rows, pair_rows = [[r[o] for o in order] for r in (mine_rows, pair_rows)]
    coefficients = first_levels(rhs_me, rows, pair_rows, [coefficients] + values)
    other = swapped(coefficients, "leaf", top)
    near.append(near_field(near_index, near_count, near_blocks, fields, half, half, [coefficients]))
    own = last_level(rhs_me, rows, pair_rows, coefficients, other, near[1:])

    def add_far(base, known, last=False):
        ids = [o * group + j for j in sorted(known) for o in range(outer)]
        blocks = []
        for j in sorted(known):
            blocks += [known[j]] + [swapped(known[j], "leaf", o * group) for o in range(1, outer)]
        return far_field(ids, tag, field_basis, base, blocks, last)

    known = {0: own[0], top: own[1]}
    total = near
    high = mid
    from_low = {j ^ low: swapped(v, "leaf", low) for j, v in known.items()}
    from_high = {j ^ high: swapped(v, "leaf", high) for j, v in known.items()}
    total = [add_far(total, known)]
    rest = {
        low ^ high: swapped(from_high[high], "leaf", low),
        top ^ low ^ high: swapped(from_low[top ^ low], "leaf", high),
    }
    total = [add_far(total, from_low | from_high)]
    total = [add_far(total, {low ^ high: rest[low ^ high]})]
    return add_far(total, {top ^ low ^ high: rest[top ^ low ^ high]}, True)


def solution(mesh):
    in_specs = (
        P("leaf", "rhs"),
        P("leaf", None),
        P("leaf", None),
        P("leaf", None),
        P("leaf", None, "rhs", None),
        P("leaf", None, None, None),
        P("leaf", None),
        P("leaf"),
    )
    out_specs = P("leaf", "rhs")
    return jax.shard_map(
        on_device, mesh=mesh, in_specs=in_specs, out_specs=out_specs, check_vma=False
    )
```

```python
import functools

import jax
import jax.numpy as jnp
from jax import lax
from jax.experimental import pallas as pl
from jax.experimental.pallas import tpu as pltpu
from jax.sharding import PartitionSpec as P

F32 = jnp.float32
BF16 = jnp.bfloat16
VMEM_LIMIT = 16 * 1024 * 1024
LANES = 128
VMEM = pl.BlockSpec(memory_space=pltpu.VMEM)
SMEM = pl.BlockSpec(memory_space=pltpu.SMEM)
HBM = pl.BlockSpec(memory_space=pltpu.HBM)
ANY = pl.BlockSpec(memory_space=pl.ANY)


def call(kernel, out_shape, values, in_specs, out_spaces, scratch=(), after=()):
    def placed(value, spec):
        space = spec.memory_space
        pinned = space in (pltpu.VMEM, pltpu.HBM)
        return pltpu.with_memory_space_constraint(value, space) if pinned else value

    return pl.pallas_call(
        kernel,
        out_shape=[space(s.shape, s.dtype) for s, space in zip(out_shape, out_spaces)],
        in_specs=list(in_specs) + [ANY if v.ndim > 1 else SMEM for v in after],
        out_specs=[pl.BlockSpec(memory_space=space) for space in out_spaces],
        scratch_shapes=list(scratch),
        compiler_params=pltpu.CompilerParams(vmem_limit_bytes=VMEM_LIMIT),
        cost_estimate=pl.CostEstimate(flops=1024, bytes_accessed=1024, transcendentals=0),
    )(*[placed(v, s) for v, s in zip(values, in_specs)], *after)


def tie(*values):
    return lax.optimization_barrier(values)


def swapped(value, axis, mask):
    return lax.ppermute(value, axis, [(i, i ^ mask) for i in range(lax.axis_size(axis))])


def products(relative, basis_t, fields, groups, outs):
    for out, group in zip(outs, groups):
        for i, j in enumerate(group):
            masked = jnp.where(relative == j, basis_t, jnp.zeros((), BF16))
            out[i] = jnp.dot(masked, fields, preferred_element_type=F32).astype(out.dtype)


def staged_compress_kernel(groups, me_ref, owner_hbm, basis_hbm, fields_hbm, *rest):
    rest = rest[-len(groups) - 4 :]
    outs, (owner_ref, basis_ref, fields_ref, sems) = rest[: len(groups)], rest[len(groups) :]
    pairs = ((owner_hbm, owner_ref), (basis_hbm, basis_ref), (fields_hbm, fields_ref))
    copies = [
        pltpu.make_async_copy(source, target, sems.at[k]) for k, (source, target) in enumerate(pairs)
    ]
    for copy in copies:
        copy.start()
    copies[0].wait()
    relative = owner_ref[...] ^ me_ref[0]
    copies[1].wait()
    basis_t = basis_ref[...].T
    copies[2].wait()
    products(relative, basis_t, fields_ref[...], groups, outs)


def compress_kernel(groups, me_ref, owner_ref, basis_ref, fields_ref, *rest):
    outs = rest[-len(groups) :]
    products(owner_ref[...] ^ me_ref[0], basis_ref[...].T, fields_ref[...], groups, outs)


def tagged_compress_kernel(groups, me_ref, owner_ref, basis_ref, fields_ref, *rest):
    outs, tag_ref = rest[-len(groups) - 1 : -1], rest[-1]
    relative = owner_ref[...] ^ me_ref[0]
    products(relative, basis_ref[...].T, fields_ref[...], groups, outs)
    wide = jnp.broadcast_to(relative.astype(F32), (LANES, relative.shape[1]))
    tag_ref[...] = wide.T.astype(BF16)


def compress(me, owner_row, basis, fields, groups, dtypes, kind, after=()):
    rows, cols = fields.shape
    width = basis.shape[1]
    staged = kind is staged_compress_kernel
    held = [
        pltpu.VMEM((1, rows), jnp.int32),
        pltpu.VMEM((rows, width), BF16),
        pltpu.VMEM((rows, cols), BF16),
        pltpu.SemaphoreType.DMA((3,)),
    ]
    shapes = [jax.ShapeDtypeStruct((len(g), width, cols), d) for g, d in zip(groups, dtypes)]
    if kind is tagged_compress_kernel:
        shapes.append(jax.ShapeDtypeStruct((rows, LANES), BF16))
    return list(
        call(
            functools.partial(kind, groups),
            shapes,
            (me, owner_row, basis, fields),
            [SMEM] + [HBM if staged else VMEM] * 3,
            [pltpu.VMEM] * len(shapes),
            held if staged else (),
            after,
        )
    )


def near_kernel(first, index_ref, count_ref, blocks_hbm, fields_ref, *rest):
    near_ref, blocks_ref, sems = rest[-3:]
    groups, slots, size, _ = blocks_ref.shape
    copies = [
        pltpu.make_async_copy(blocks_hbm.at[first + g], blocks_ref.at[g], sems.at[g])
        for g in range(groups)
    ]
    for copy in copies:
        copy.start()
    for g, copy in enumerate(copies):
        chosen = []
        for j in range(slots):
            start = pl.multiple_of(index_ref[first + g, j] * size, size)
            piece = fields_ref[pl.ds(start, size), :]
            live = j < count_ref[first + g]
            chosen.append(jnp.where(live, piece, jnp.zeros_like(piece)))
        copy.wait()
        weights = jnp.concatenate([blocks_ref[g, j] for j in range(slots)], axis=1)
        near_ref[g * size : (g + 1) * size, :] = jnp.dot(
            weights, jnp.concatenate(chosen, axis=0), preferred_element_type=F32
        )


def near_field(near_index, near_count, near_blocks, fields, first, groups, after):
    _, slots, size, _ = near_blocks.shape
    (near,) = call(
        functools.partial(near_kernel, first),
        [jax.ShapeDtypeStruct((groups * size, fields.shape[1]), F32)],
        (near_index, near_count, near_blocks, fields),
        [SMEM, SMEM, HBM, VMEM],
        [pltpu.VMEM],
        [pltpu.VMEM((groups, slots, size, size), BF16), pltpu.SemaphoreType.DMA((groups,))],
        after,
    )
    return near


def apply_rows(me, pieces, stacked, out):
    product = jnp.dot(jnp.concatenate(pieces, axis=0), stacked, preferred_element_type=F32)
    size = pieces[0].shape[0]
    for o in range(len(pieces)):
        start = pl.multiple_of((me ^ o) * size, size)
        out[pl.ds(start, size), :] = product[o * size : (o + 1) * size].astype(out.dtype)


def first_levels_kernel(n_rhs, me_ref, *refs):
    rows, pair_rows = refs[:n_rhs], refs[n_rhs : 2 * n_rhs]
    own_ref, low_ref, mid_ref, both_ref, out_ref, held_ref = refs[2 * n_rhs :]
    stacked = jnp.concatenate([own_ref[...], low_ref[...]], axis=0)
    apply_rows(me_ref[0], [ref[0] for ref in rows], stacked, held_ref.at[0])
    stacked = jnp.concatenate([mid_ref[...], both_ref[...]], axis=0)
    apply_rows(me_ref[0], [ref[0] for ref in pair_rows], stacked, held_ref.at[1])
    stacked = jnp.concatenate([held_ref[0], held_ref[1]], axis=0)
    apply_rows(me_ref[0], [ref[1] for ref in rows], stacked, out_ref)


def first_levels(rhs_me, rows, pair_rows, values):
    shape = values[0].shape
    (out,) = call(
        functools.partial(first_levels_kernel, len(rows)),
        [jax.ShapeDtypeStruct(shape, BF16)],
        (rhs_me, *rows, *pair_rows, *values),
        [SMEM] + [VMEM] * (2 * len(rows) + len(values)),
        [pltpu.VMEM],
        [pltpu.VMEM((2,) + shape, BF16)],
    )
    return out


def last_level_kernel(n_rhs, me_ref, *refs):
    rows, pair_rows = refs[:n_rhs], refs[n_rhs : 2 * n_rhs]
    own, other = [ref[...] for ref in refs[2 * n_rhs :][:2]]
    level = rows[0].shape[0] - 1
    stacked = jnp.concatenate([own, other], axis=0)
    apply_rows(me_ref[0], [ref[level] for ref in rows], stacked, refs[-2])
    stacked = jnp.concatenate([other, own], axis=0)
    apply_rows(me_ref[0], [ref[1] for ref in pair_rows], stacked, refs[-1])


def last_level(rhs_me, rows, pair_rows, own, other, after):
    return call(
        functools.partial(last_level_kernel, len(rows)),
        [jax.ShapeDtypeStruct(own.shape, BF16)] * 2,
        (rhs_me, *rows, *pair_rows, own, other),
        [SMEM] + [VMEM] * (2 * len(rows) + 2),
        [pltpu.VMEM] * 2,
        (),
        after,
    )


def far_tile(ids, tag_ref, basis_ref, bases, blocks, start, tile):
    part = pl.ds(start, tile)
    rows = bases[0].shape[0]
    base = bases[start // rows][pl.ds(start % rows, tile), :]
    tag = tag_ref[part, :]
    basis = basis_ref[part, :]
    lanes = [basis[:, k : k + LANES] for k in range(0, basis.shape[1], LANES)]
    masked = [jnp.where(tag == j, piece, jnp.zeros((), BF16)) for j in ids for piece in lanes]
    stacked = [ref[...] for ref in blocks]
    total = jnp.dot(
        jnp.concatenate(masked, axis=1),
        jnp.concatenate(stacked, axis=0),
        preferred_element_type=F32,
    )
    return total.astype(BF16).astype(F32) + base


def far_kernel(ids, tile, n_base, tag_ref, basis_ref, *refs):
    bases, blocks, out_ref = refs[:n_base], refs[n_base:-1], refs[-1]
    for start in range(0, out_ref.shape[0], tile):
        value = far_tile(ids, tag_ref, basis_ref, bases, blocks, start, tile)
        out_ref[pl.ds(start, tile), :] = value


def last_far_kernel(ids, tile, n_base, tag_ref, basis_ref, *refs):
    bases, blocks, (out_hbm, held_ref, sems) = refs[:n_base], refs[n_base:-3], refs[-3:]
    copies = []
    for t in range(out_hbm.shape[0] // tile):
        value = far_tile(ids, tag_ref, basis_ref, bases, blocks, t * tile, tile)
        part = pl.ds(t * tile, tile)
        held_ref[part, :] = value.astype(BF16)
        copies.append(pltpu.make_async_copy(held_ref.at[part], out_hbm.at[part], sems.at[t]))
        copies[-1].start()
    for copy in copies:
        copy.wait()


def far_field(ids, tag, basis, bases, blocks, last=False):
    rows, cols = basis.shape[0], bases[0].shape[1]
    tile = min(bases[0].shape[0], 512)
    held = [pltpu.VMEM((rows, cols), BF16), pltpu.SemaphoreType.DMA((rows // tile,))]
    (out,) = call(
        functools.partial(last_far_kernel if last else far_kernel, ids, tile, len(bases)),
        [jax.ShapeDtypeStruct((rows, cols), BF16 if last else F32)],
        (tag, basis, *bases, *blocks),
        [VMEM] * (2 + len(bases) + len(blocks)),
        [pltpu.HBM if last else pltpu.VMEM],
        held if last else (),
    )
    return out


def across(pieces, mask):
    while mask:
        pieces = pieces | {o ^ mask: swapped(v, "rhs", mask) for o, v in pieces.items()}
        mask //= 2
    return pieces


def on_device(
    fields, owner, source_basis, field_basis, transfer, near_blocks, near_index, near_count
):
    n_leaf = lax.axis_size("leaf")
    rows, cols = fields.shape
    levels = transfer.shape[1]
    group = 2**levels
    outer = n_leaf // group
    upper = group // 2
    n_rhs = lax.axis_size("rhs")
    me = lax.axis_index("leaf").astype(jnp.int32)[None]
    rhs_me = lax.axis_index("rhs").astype(jnp.int32)[None]
    owner_row = owner.reshape(1, rows)

    parts = [list(range(upper - 1, upper // 2 - 1, -1)), list(range(upper // 2 - 1, -1, -1))]

    def groups(low):
        return [[o * group + 2 * s + low for s in part for o in range(outer)] for part in parts]

    odd, even = groups(1), groups(0)
    operands = (me, owner_row, source_basis)
    (send,) = compress(*operands, fields, odd[:1], [BF16], staged_compress_kernel, [rhs_me])
    fields, send = tie(fields, send)
    got = [swapped(send, "leaf", 1)]
    *keep, send = compress(*operands, fields, [even[0], odd[1]], [F32, BF16], compress_kernel)
    got.append(swapped(send, "leaf", 1))

    def reduced(keep, got, part):
        total = keep + got.astype(F32)
        sums = []
        for i in range(len(part)):
            mine = total[i * outer]
            for o in range(1, outer):
                piece = total[i * outer + o].astype(BF16)
                mine = mine + swapped(piece, "leaf", o * group).astype(F32)
            sums.append(mine)
        return sums

    transfer, keep[0] = tie(transfer, keep[0])
    low, mid, top = 1, 2, group // 2
    far_rhs = n_rhs // 2
    mine_rows = {0: transfer[0], far_rhs: swapped(transfer[0], "rhs", far_rhs)}
    pair = [swapped(transfer[0, 0], "leaf", mid), swapped(transfer[0, -1], "leaf", top)]

    sums = [v.astype(BF16) for v in reduced(keep[0], got[0], parts[0])]
    arrived = [swapped(v, "leaf", 2 * s) for s, v in zip(parts[0], sums)]
    more, tag = compress(*operands, fields, even[1:], [F32], tagged_compress_kernel, sums[:1])
    got[1], mine_rows[0], mine_rows[far_rhs], *pair = tie(
        got[1], mine_rows[0], mine_rows[far_rhs], *pair
    )
    pair_rows = {0: jnp.stack(pair)}
    pair_rows[far_rhs] = swapped(pair_rows[0], "rhs", far_rhs)
    *near_sums, total = reduced(more, got[1], parts[1])
    for s, v in zip(parts[1], near_sums):
        arrived.append(swapped(v.astype(BF16), "leaf", 2 * s))
    half = near_blocks.shape[0] // 2
    near = [near_field(near_index, near_count, near_blocks, fields, 0, half, sums[:1])]
    mine_rows = across(mine_rows, far_rhs // 2)
    order = sorted(mine_rows)
    total, near[0], pair_rows[far_rhs] = tie(total, near[0], pair_rows[far_rhs])

    for value in arrived[len(sums) :] + arrived[: len(sums)]:
        total = total + value.astype(F32)
    coefficients = total.astype(BF16)
    values = [swapped(coefficients, "leaf", mask) for mask in (low, mid, low ^ mid)]
    pair_rows = across(pair_rows, far_rhs // 2)
    rows, pair_rows = [[r[o] for o in order] for r in (mine_rows, pair_rows)]
    coefficients = first_levels(rhs_me, rows, pair_rows, [coefficients] + values)
    other = swapped(coefficients, "leaf", top)
    near.append(near_field(near_index, near_count, near_blocks, fields, half, half, [coefficients]))
    own = last_level(rhs_me, rows, pair_rows, coefficients, other, near[1:])

    def add_far(base, known, last=False):
        ids = [o * group + j for j in sorted(known) for o in range(outer)]
        blocks = []
        for j in sorted(known):
            blocks += [known[j]] + [swapped(known[j], "leaf", o * group) for o in range(1, outer)]
        return far_field(ids, tag, field_basis, base, blocks, last)

    known = {0: own[0], top: own[1]}
    total = near
    high = mid
    from_high = {j ^ high: swapped(v, "leaf", high) for j, v in known.items()}
    from_low = {j ^ low: swapped(v, "leaf", low) for j, v in reversed(known.items())}
    total = [add_far(total, known)]
    rest = {
        low ^ high: swapped(from_high[high], "leaf", low),
        top ^ low ^ high: swapped(from_low[top ^ low], "leaf", high),
    }
    total = [add_far(total, from_low | from_high)]
    return add_far(total, rest, True)


def solution(mesh):
    in_specs = (
        P("leaf", "rhs"),
        P("leaf", None),
        P("leaf", None),
        P("leaf", None),
        P("leaf", None, "rhs", None),
        P("leaf", None, None, None),
        P("leaf", None),
        P("leaf"),
    )
    out_specs = P("leaf", "rhs")
    return jax.shard_map(
        on_device, mesh=mesh, in_specs=in_specs, out_specs=out_specs, check_vma=False
    )
```
